512 devices in a mesh: grad: 32 (over y, z_hi), dp: 16 (over x, z_lo, core).
Axes of the slice: x: 4, y: 8, z: 8 (z_hi: 4, z_lo: 2; z = z_hi * 2 + z_lo), core: 2. Of those that a mesh axis runs over, the one named last changes fastest.
Arguments:
- gradient: bfloat16 [32, 512, 5120], P('grad', 'dp'), may hold values from -6 to 6
- out_bases: bfloat16 [32, 512, 512], P('grad'), may hold values from -0.25 to 0.25
- in_bases: bfloat16 [32, 512, 512], P('grad'), may hold values from -0.25 to 0.25
- out_values: float32 [32, 512], P('grad'), may hold values from 0.3 to 3
- in_values: float32 [2, 5120], replicated, may hold values from 0.3 to 3
- block_layer: int32 [32], P('grad'), may hold values from 0 to 1
- in_owner: int32 [2, 10], replicated, may hold values from 0 to 31, as said below
Outputs:
- preconditioned: bfloat16 [32, 512, 5120], P('grad', 'dp')
The draws below stay inside these ranges and needn't reach their ends.
Inputs may be any that keep to these rules, and one draw needn't show every extreme that they name: `in_owner`: entries are distinct; entry (l, j) names slot s of the stored bases, held by gradient worker s // 1 as its local slot s % 1.
All inputs are finite; a program needn't handle non-finite values.
Results may differ from the reference program's by a relative error of at most 0.0055.
Values may be sent and summed in bfloat16 or wider, within the bound.
A program may use at most 64 MiB of HBM per device.

```python
import math
import jax
import jax.numpy as jnp
from jax import lax

D = 5120
BLK = 512
NLAYERS = 2
KI = 10
TILE_ROWS = 32
A_SLOTS = 1
N_GRAD = 32


def draw_in_owner(key, part):
    key = jax.random.fold_in(key, 7)
    order = jax.random.permutation(key, N_GRAD * A_SLOTS)
    return order[:NLAYERS * KI].reshape(NLAYERS, KI).astype(jnp.int32)


def set_ends(values, key, smallest, high):
    shape = values.shape
    index_at = [jax.random.randint(jax.random.fold_in(key, axis), (), 0, shape[axis]) for axis in range(len(shape))]
    values = values.at[tuple(index_at)].set(smallest)
    longest = shape.index(max(shape))
    index_at[longest] = (index_at[longest] + 1) % shape[longest]
    return values.at[tuple(index_at)].set(high)


def block_scale(rng, shape, shards, least, high):
    def one(dim, parts):
        draws = jax.random.uniform(jax.random.fold_in(jax.random.fold_in(rng, 6), dim), (parts,), jnp.float32, least / len(shards), high / len(shards))
        return jnp.repeat(jnp.exp(draws), shape[dim] // parts).reshape((-1,) + (1,) * (len(shape) - dim - 1))

    loudness = one(*shards[0])
    for cut in shards[1:]:
        loudness = loudness * one(*cut)
    return loudness


def noise(own_key, dims, deviation, reach, split=(), held_as=jnp.bfloat16):
    values = jax.random.normal(own_key, dims, jnp.float32) * deviation
    if len(split) > 0:
        values = block_scale(own_key, dims, split, -0.22, 0.18) * values
    return jnp.clip(values, min=-reach, max=reach).astype(held_as)


def setup_inputs(seed: int = 0) -> dict:
    keys = jax.random.split(jax.random.key(seed), 8)
    return {
        "gradient": noise(keys[0], (TILE_ROWS, BLK, D), 1.0, 6.0, ((0, 32), (1, 16))),
        "out_bases": noise(keys[1], (TILE_ROWS, BLK, BLK), BLK ** -0.5, 0.25, ((0, 32),)),
        "in_bases": noise(keys[2], (N_GRAD * A_SLOTS, BLK, BLK), BLK ** -0.5, 0.25, ((0, 32),)),
        "out_values": jnp.clip(jnp.exp(math.log(3.0) - 2.3025851 * jax.random.uniform(keys[3], (TILE_ROWS, BLK), jnp.float32) ** block_scale(keys[3], (TILE_ROWS, BLK), ((0, 32),), -0.2, 0.2)), 0.3, 3.0),
        "in_values": jnp.clip(jnp.exp(jax.random.uniform(keys[4], (NLAYERS, D), jnp.float32, math.log(0.3), math.log(3.0))), 0.3, 3.0),
        "block_layer": set_ends(jax.random.randint(keys[5], (TILE_ROWS,), 0, NLAYERS), jax.random.fold_in(keys[5], 1), 0, NLAYERS - 1).astype(jnp.int32),
        "in_owner": draw_in_owner(jax.random.fold_in(keys[7], 71), 0),
    }


DAMPING = 0.1


def reference(gradient, out_bases, in_bases, out_values, in_values, block_layer, in_owner):
    block_count = D // BLK
    in_tiles = jnp.take(in_bases, in_owner.reshape(-1), axis=0).reshape(NLAYERS, block_count, BLK, BLK)
    wide_tiles = in_tiles.astype(jnp.float32)

    def one_block(items):
        grad_rows, basis, values, layer_index = items
        layer_tiles = lax.dynamic_index_in_dim(wide_tiles, layer_index, 0, keepdims=False)
        layer_values = lax.dynamic_index_in_dim(in_values, layer_index, 0, keepdims=False)
        blocked = grad_rows.reshape(BLK, block_count, BLK).astype(jnp.float32)
        projected = jnp.einsum("rjk,jkc->rjc", blocked, layer_tiles).astype(jnp.bfloat16).reshape(BLK, D)
        moments = jnp.dot(basis.T, projected, preferred_element_type=jnp.float32)
        scaled = (moments / (values[:, None] * layer_values[None, :] + DAMPING)).astype(jnp.bfloat16)
        mixed_rows = jnp.dot(basis, scaled, preferred_element_type=jnp.float32).astype(jnp.bfloat16)
        blocked_mix = mixed_rows.reshape(BLK, block_count, BLK).astype(jnp.float32)
        result = jnp.einsum("rjc,jkc->rjk", blocked_mix, layer_tiles).astype(jnp.bfloat16)
        return result.reshape(BLK, D)

    return lax.map(one_block, (gradient, out_bases, out_values, block_layer))
```

```python
import jax
import jax.numpy as jnp
from jax import lax
from jax.experimental import pallas as pl
from jax.experimental.pallas import tpu as pltpu
from jax.sharding import PartitionSpec as P

DAMPING = 0.1
MESH = pl.DeviceIdType.MESH
ZN = 4
RIGHT, LEFT = 0, 1


def owner_device(j):
    return jnp.where(j < 8, 2 * j, jnp.where(j == 8, 1, 11))


def owned_block(p):
    return jnp.where(p % 2 == 0, p // 2, jnp.where(p == 1, 8, 9))


def hops(direction, k):
    if direction == RIGHT:
        return 4 if k < 2 else 3
    return 3 if k < 2 else 4


def dot(a, b, contract):
    return lax.dot_general(a, b, (contract, ((), ())), preferred_element_type=jnp.float32)


def kernel(
    yn, pn, jn,
    owner_ref, layer_ref, grad_ref, ob_ref, ib_ref, ov_ref, iv_ref,
    out_ref,
    obuf, obt, gbuf, ybuf, rbuf, tall, tsend, tbuf, sbuf, res,
    lsem, zs, zr, ys, yr, gs, gr, ts, tr, ms, mr,
):
    g = lax.axis_index("grad")
    p = lax.axis_index("dp")
    y, zh = g // ZN, g % ZN
    rows = grad_ref.shape[1]
    blk = ob_ref.shape[1]
    own_rows = pl.ds(pl.multiple_of(p * rows, rows), rows)
    active = (p % 2 == 0) | (p == 1) | (p == 11)
    mine = owned_block(p)

    def remote(src, dst, ssem, rsem, gg, pp):
        return pltpu.make_async_remote_copy(
            src_ref=src, dst_ref=dst, send_sem=ssem, recv_sem=rsem, device_id=(gg, pp), device_id_type=MESH
        )

    def slot(yy, k):
        return lax.rem(yy + 2 * yn, yn) * ZN + lax.rem(zh - k + ZN, ZN)

    load_basis = pltpu.make_async_copy(ob_ref.at[0], obuf, lsem.at[0])
    load_strip = pltpu.make_async_copy(ib_ref.at[0, own_rows, :], tall.at[g], lsem.at[1])
    load_basis.start()
    load_strip.start()

    zpeer = [y * ZN + lax.rem(zh + k, ZN) for k in range(ZN)]
    ypeer = (lax.rem(y + 1, yn) * ZN + zh, lax.rem(y + yn - 1, yn) * ZN + zh)

    barrier = pltpu.get_barrier_semaphore()
    for i in range(1, pn):
        pl.semaphore_signal(barrier, inc=1, device_id=(g, lax.rem(p + i, pn)), device_id_type=MESH)
    for k in range(1, ZN):
        pl.semaphore_signal(barrier, inc=1, device_id=(zpeer[k], p), device_id_type=MESH)
    for d in (RIGHT, LEFT):
        pl.semaphore_signal(barrier, inc=1, device_id=(ypeer[d], p), device_id_type=MESH)
    pl.semaphore_wait(barrier, pn - 1 + ZN - 1 + 2)

    zcopy = {}
    for k in (1, 3, 2):
        zcopy[k] = remote(ib_ref.at[0, own_rows, :], tall.at[g], zs.at[k - 1], zr.at[k - 1], zpeer[k], p)
        zcopy[k].start()

    def ycopy(d, hop, k):
        origin = y - hop if d == RIGHT else y + hop
        s = slot(origin, k)
        src = ib_ref.at[0, own_rows, :] if hop == 0 and k == 0 else tall.at[s]
        return remote(src, tall.at[s], ys.at[d, hop, k], yr.at[d, hop, k], ypeer[d], p)

    for d in (RIGHT, LEFT):
        ycopy(d, 0, 0).start()

    def gcopy(i):
        j = lax.rem(i + p, jn)
        return j, remote(
            grad_ref.at[0, :, pl.ds(pl.multiple_of(j * blk, blk), blk)],
            gbuf.at[own_rows, :], gs.at[i], gr, g, owner_device(j),
        )

    for i in range(jn):
        j, copy = gcopy(i)

        @pl.when(owner_device(j) != p)
        def _():
            copy.start()

    @pl.when(active)
    def _():
        pltpu.make_async_copy(
            grad_ref.at[0, :, pl.ds(pl.multiple_of(mine * blk, blk), blk)], gbuf.at[own_rows, :], gr
        ).start()

    layer = layer_ref[0]
    load_basis.wait()

    @pl.when(active)
    def _():
        obt[...] = obuf[...].T
        spread = jnp.broadcast_to(ov_ref[...], (128, blk)).T
        for c in range(0, blk, 128):
            values = iv_ref[:, pl.ds(pl.multiple_of(mine * blk + c, 128), 128)]
            values = jnp.where(layer == 0, values[0:1], values[1:2])
            rbuf[:, c : c + 128] = 1.0 / (spread * values + DAMPING)

    load_strip.wait()
    for k in (1, 3, 2):
        zcopy[k].wait_recv()
        for d in (RIGHT, LEFT):
            ycopy(d, 0, k).start()

    def project(lo, size):
        @pl.when(active)
        def _():
            if lo == 0:
                pltpu.make_async_copy(gbuf, gbuf, gr).wait()
            ybuf[lo : lo + size, :] = dot(obt[lo : lo + size, :], gbuf[...], ((1,), (0,))).astype(jnp.bfloat16)

    order = (0, 1, 3, 2)
    for hop in range(1, 5):
        for n, k in enumerate(order):
            for d in (RIGHT, LEFT):
                if hop <= hops(d, k):
                    ycopy(d, hop - 1, k).wait_recv()
                    if hop < hops(d, k):
                        ycopy(d, hop, k).start()
            if hop == 2:
                project(n * (blk // 4), blk // 4)

    def tcopy(i):
        j = lax.rem(i + p, jn)
        return j, remote(tsend.at[j], tbuf.at[own_rows, :], ts.at[i], tr, g, owner_device(j))

    for i in range(jn):
        j, copy = tcopy(i)
        tsend[j] = tall[owner_ref[layer, j]]

        @pl.when(owner_device(j) != p)
        def _():
            copy.start()

    def mcopy(i, base):
        dest = base + i
        strip = pl.ds(pl.multiple_of(dest * rows, rows), rows)
        cols = pl.ds(pl.multiple_of(mine * blk, blk), blk)
        return dest, res.at[strip, :], out_ref.at[0, :, cols]

    half = blk // 2
    per_half = pn // 2

    @pl.when(active)
    def _():
        pltpu.make_async_copy(tsend.at[mine], tbuf.at[own_rows, :], tr).start()
        pltpu.make_async_copy(tbuf, tbuf, tr).wait()
        for lo in (0, half):
            moments = dot(ybuf[lo : lo + half, :], tbuf[...], ((1,), (0,)))
            sbuf[lo : lo + half, :] = (moments * rbuf[lo : lo + half, :]).astype(jnp.bfloat16)
        for lo in (0, 1):
            part = slice(lo * half, lo * half + half)
            mixed = dot(obuf[part, :], sbuf[...], ((1,), (0,))).astype(jnp.bfloat16)
            res[part, :] = dot(mixed, tbuf[...], ((1,), (1,))).astype(jnp.bfloat16)
            for i in range(per_half):
                dest, src, dst = mcopy(i, lo * per_half)

                @pl.when(dest != p)
                def _():
                    remote(src, dst, ms.at[dest], mr, g, dest).start()

                @pl.when(dest == p)
                def _():
                    pltpu.make_async_copy(src, dst, mr).start()

    pltpu.make_async_copy(out_ref.at[0], out_ref.at[0], mr).wait()

    for k in (1, 3, 2):
        zcopy[k].wait_send()
    for d in (RIGHT, LEFT):
        for k in range(ZN):
            for hop in range(hops(d, k)):
                ycopy(d, hop, k).wait_send()
    for i in range(jn):
        j, copy = gcopy(i)
        _, other = tcopy(i)

        @pl.when(owner_device(j) != p)
        def _():
            copy.wait_send()
            other.wait_send()

    @pl.when(active)
    def _():
        for i in range(pn):
            dest, src, dst = mcopy(i, 0)

            @pl.when(dest != p)
            def _():
                remote(src, dst, ms.at[dest], mr, g, dest).wait_send()


def solution(mesh):
    yn = mesh.shape["grad"] // ZN
    pn = mesh.shape["dp"]

    def shards(gradient, out_bases, in_bases, out_values, in_values, block_layer, in_owner):
        rows, width = gradient.shape[1:]
        blk = out_bases.shape[1]
        jn = width // blk
        slots = yn * ZN
        bf16, f32 = jnp.bfloat16, jnp.float32
        any_spec = pl.BlockSpec(memory_space=pl.ANY)
        smem = pl.BlockSpec(memory_space=pltpu.SMEM)
        vmem = pl.BlockSpec(memory_space=pltpu.VMEM)
        dma = pltpu.SemaphoreType.DMA

        def body(*refs):
            kernel(yn, pn, jn, *refs)

        return pl.pallas_call(
            body,
            out_shape=jax.ShapeDtypeStruct(gradient.shape, bf16),
            in_specs=[smem, smem, any_spec, any_spec, any_spec, vmem, vmem],
            out_specs=any_spec,
            scratch_shapes=[
                pltpu.VMEM((blk, blk), bf16),
                pltpu.VMEM((blk, blk), bf16),
                pltpu.VMEM((blk, blk), bf16),
                pltpu.VMEM((blk, blk), bf16),
                pltpu.VMEM((blk, blk), f32),
                pltpu.VMEM((slots, rows, blk), bf16),
                pltpu.VMEM((jn, rows, blk), bf16),
                pltpu.VMEM((blk, blk), bf16),
                pltpu.VMEM((blk, blk), bf16),
                pltpu.VMEM((blk, blk), bf16),
                dma((2,)),
                dma((ZN - 1,)),
                dma((ZN - 1,)),
                dma((2, 4, ZN)),
                dma((2, 4, ZN)),
                dma((jn,)),
                dma,
                dma((jn,)),
                dma,
                dma((pn,)),
                dma,
            ],
            compiler_params=pltpu.CompilerParams(
                collective_id=0, has_side_effects=True, vmem_limit_bytes=32 * 1024 * 1024
            ),
        )(in_owner, block_layer, gradient, out_bases, in_bases, out_values, in_values)

    in_specs = (
        P("grad", "dp", None),
        P("grad", None, None),
        P("grad", None, None),
        P("grad", None),
        P(),
        P("grad"),
        P(),
    )
    return jax.shard_map(shards, mesh=mesh, in_specs=in_specs, out_specs=P("grad", "dp", None), check_vma=False)
```

```python
import jax
import jax.numpy as jnp
from jax import lax
from jax.experimental import pallas as pl
from jax.experimental.pallas import tpu as pltpu
from jax.sharding import PartitionSpec as P

DAMPING = 0.1
MESH = pl.DeviceIdType.MESH
ZN = 4
RIGHT, LEFT = 0, 1
SCHEME = ("skip", "skip", "skip", "skip")
ORDER = (
    ("y", 0, 1), ("prepare", 0), ("up", 1, "first"), ("y", 0, 2), ("prepare", 1), ("z", 1), ("up", 1, "rest"),
    ("up", 2, "all"), ("up", 3, "all"), ("prepare", 2), ("y", 0, 3), ("prepare", 3), ("y", 0, 4), ("z", 2), ("z", 3),
    ("y", 1, 1), ("y", 1, 2), ("project", 0), ("y", 2, 1), ("y", 2, 2), ("project", 1), ("y", 3, 1), ("y", 3, 2),
    ("project", 2), ("y", 1, 3), ("y", 1, 4), ("project", 3), ("y", 2, 3), ("y", 2, 4), ("y", 3, 3), ("y", 3, 4),
)


def owner_device(j):
    return jnp.where(j < 8, 2 * j, jnp.where(j == 8, 1, 11))


def owned_block(p):
    return jnp.where(p % 2 == 0, p // 2, jnp.where(p == 1, 8, 9))


def reach(direction, c):
    return 4 if (c < 2) == (direction == RIGHT) else 3


def eval_where(which, zh):
    return zh % 2 == 0 if which == "first" else zh % 2 == 1 if which == "rest" else True


def dot(a, b, contract):
    return lax.dot_general(a, b, (contract, ((), ())), preferred_element_type=jnp.float32)


def kernel(
    yn, pn, jn,
    owner_in, layer_in, grad_ref, ob_ref, ib_ref, ov_ref, iv_ref,
    out_ref,
    owner_ref, layer_ref, obuf, obt, gbuf, ybuf, rbuf, tall, tsend, tbuf, sbuf, res,
    lsem, zready, zs, zr, ys, yr, gs, gr, ts, tr, ms, mr,
):
    g = lax.axis_index("grad")
    p = lax.axis_index("dp")
    y, zh = g // ZN, g % ZN
    rows = grad_ref.shape[1]
    blk = ob_ref.shape[1]
    own_rows = pl.ds(pl.multiple_of(p * rows, rows), rows)
    active = (p % 2 == 0) | (p == 1) | (p == 11)
    mine = owned_block(p)

    def remote(src, dst, ssem, rsem, gg, pp):
        return pltpu.make_async_remote_copy(
            src_ref=src, dst_ref=dst, send_sem=ssem, recv_sem=rsem, device_id=(gg, pp), device_id_type=MESH
        )

    def zpeer(k):
        return y * ZN + lax.rem(zh + k + ZN, ZN)

    def ypeer(d):
        return lax.rem(y + d + yn, yn) * ZN + zh

    def slot(d, k):
        return lax.rem(y + d + yn, yn) * ZN + lax.rem(zh - k + ZN, ZN)

    loads = [
        pltpu.make_async_copy(src, dst, lsem.at[i])
        for i, (src, dst) in enumerate(
            ((ib_ref.at[0, own_rows, :], tall.at[g]), (ob_ref.at[0], obuf), (owner_in, owner_ref), (layer_in, layer_ref))
        )
    ]
    load_strip, load_basis, load_owner, load_layer = loads
    for load in loads:
        load.start()

    barrier = pltpu.get_barrier_semaphore()
    for k in (3, 2, 1):
        @pl.when(zh + k < ZN)
        def _():
            pl.semaphore_signal(barrier, inc=1, device_id=(zpeer(k), p), device_id_type=MESH)
    for d in (1, -1, 2, -2):
        pl.semaphore_signal(barrier, inc=1, device_id=(ypeer(d), p), device_id_type=MESH)
    for i in range(1, pn):
        pl.semaphore_signal(barrier, inc=1, device_id=(g, lax.rem(p + i, pn)), device_id_type=MESH)
    pl.semaphore_wait(barrier, pn - 1 + 4 + zh)
    for k in (1, 2, 3):
        @pl.when(zh - k >= 0)
        def _():
            pl.semaphore_signal(zready.at[k - 1], inc=1, device_id=(zpeer(-k), p), device_id_type=MESH)

    def zcopy(k):
        return remote(ib_ref.at[0, own_rows, :], tall.at[g], zs.at[k - 1], zr.at[k - 1], zpeer(k), p)

    def zup(k, where=True):
        @pl.when((zh + k < ZN) & where)
        def _():
            pl.semaphore_wait(zready.at[k - 1], 1)
            zcopy(k).start()

    for k in (1, 3, 2):
        @pl.when(zh + k >= ZN)
        def _():
            zcopy(k).start()

    first = jnp.where(zh % 2 == 0, 3, 1)
    kinds = (0, first, 4 - first, 2)

    def ycopy(d, c, here, there):
        sign = 1 if d == RIGHT else -1
        s = slot(-sign * here, kinds[c])
        src = ib_ref.at[0, own_rows, :] if here == 0 and c == 0 else tall.at[s]
        return remote(src, tall.at[s], ys.at[d, there - 1, c], yr.at[d, there - 1, c], ypeer(sign * (there - here)), p)

    def onward(c, here):
        for d in (RIGHT, LEFT):
            for there in range(here + 1, reach(d, c) + 1):
                if SCHEME[c] == "chain":
                    go = there == here + 1
                else:
                    go = here in (0, 2) and there <= here + 2
                if go:
                    ycopy(d, c, here, there).start()

    def zgot(c):
        pltpu.make_async_copy(tall.at[0], tall.at[0], zr.at[kinds[c] - 1]).wait()
        onward(c, 0)

    def ygot(c, here):
        for d in (RIGHT, LEFT):
            if here <= reach(d, c):
                pltpu.make_async_copy(tall.at[0], tall.at[0], yr.at[d, here - 1, c]).wait()
        onward(c, here)

    onward(0, 0)

    def gcopy(i):
        j = lax.rem(i + p, jn)
        return j, remote(
            grad_ref.at[0, :, pl.ds(pl.multiple_of(j * blk, blk), blk)],
            gbuf.at[own_rows, :], gs.at[i], gr, g, owner_device(j),
        )

    for i in range(jn):
        j, copy = gcopy(i)

        @pl.when(owner_device(j) != p)
        def _():
            copy.start()

    @pl.when(active)
    def _():
        pltpu.make_async_copy(
            grad_ref.at[0, :, pl.ds(pl.multiple_of(mine * blk, blk), blk)], gbuf.at[own_rows, :], gr
        ).start()

    load_layer.wait()
    load_owner.wait()
    load_strip.wait()
    load_basis.wait()
    layer = layer_ref[0]

    def prepare(n):
        part = slice(n * (blk // 4), (n + 1) * (blk // 4))

        @pl.when(active)
        def _():
            obt[:, part] = obuf[part, :].T
            spread = jnp.broadcast_to(ov_ref[...], (blk // 4, blk)).T
            values = iv_ref[:, pl.ds(pl.multiple_of(mine * blk + n * (blk // 4), blk // 4), blk // 4)]
            values = jnp.where(layer == 0, values[0:1], values[1:2])
            rbuf[:, part] = 1.0 / (spread * values + DAMPING)

    def project(n):
        lo, size = n * (blk // 4), blk // 4

        @pl.when(active)
        def _():
            if lo == 0:
                pltpu.make_async_copy(gbuf, gbuf, gr).wait()
            ybuf[lo : lo + size, :] = dot(obt[lo : lo + size, :], gbuf[...], ((1,), (0,))).astype(jnp.bfloat16)

    for step in ORDER:
        what, n = step[0], step[1]
        if what == "up":
            zup(n, eval_where(step[2], zh))
        elif what == "z":
            zgot(n)
        elif what == "y":
            ygot(n, step[2])
        elif what == "prepare":
            prepare(n)
        else:
            project(n)

    def tcopy(i):
        j = lax.rem(i + p, jn)
        return j, remote(tsend.at[j], tbuf.at[own_rows, :], ts.at[i], tr, g, owner_device(j))

    for i in range(jn):
        j, copy = tcopy(i)
        tsend[j] = tall[owner_ref[layer, j]]

        @pl.when(owner_device(j) != p)
        def _():
            copy.start()

    def mcopy(i, base):
        dest = base + i
        strip = pl.ds(pl.multiple_of(dest * rows, rows), rows)
        cols = pl.ds(pl.multiple_of(mine * blk, blk), blk)
        return dest, res.at[strip, :], out_ref.at[0, :, cols]

    half = blk // 2
    per_half = pn // 2

    @pl.when(active)
    def _():
        pltpu.make_async_copy(tsend.at[mine], tbuf.at[own_rows, :], tr).start()
        pltpu.make_async_copy(tbuf, tbuf, tr).wait()
        for lo in (0, half):
            moments = dot(ybuf[lo : lo + half, :], tbuf[...], ((1,), (0,)))
            sbuf[lo : lo + half, :] = (moments * rbuf[lo : lo + half, :]).astype(jnp.bfloat16)
        for lo in (0, 1):
            part = slice(lo * half, lo * half + half)
            mixed = dot(obuf[part, :], sbuf[...], ((1,), (0,))).astype(jnp.bfloat16)
            res[part, :] = dot(mixed, tbuf[...], ((1,), (1,))).astype(jnp.bfloat16)
            for i in range(per_half):
                dest, src, dst = mcopy(i, lo * per_half)

                @pl.when(dest != p)
                def _():
                    remote(src, dst, ms.at[dest], mr, g, dest).start()

                @pl.when(dest == p)
                def _():
                    pltpu.make_async_copy(src, dst, mr).start()

    pltpu.make_async_copy(out_ref.at[0], out_ref.at[0], mr).wait()

    for k in (1, 2, 3):
        zcopy(k).wait_send()
    for d in (RIGHT, LEFT):
        for c in range(ZN):
            for there in range(1, reach(d, c) + 1):
                pltpu.make_async_copy(tall.at[0], tall.at[0], ys.at[d, there - 1, c]).wait()
    for i in range(jn):
        j, copy = gcopy(i)
        _, other = tcopy(i)

        @pl.when(owner_device(j) != p)
        def _():
            copy.wait_send()
            other.wait_send()

    @pl.when(active)
    def _():
        for i in range(pn):
            dest, src, dst = mcopy(i, 0)

            @pl.when(dest != p)
            def _():
                remote(src, dst, ms.at[dest], mr, g, dest).wait_send()


def solution(mesh):
    yn = mesh.shape["grad"] // ZN
    pn = mesh.shape["dp"]

    def shards(gradient, out_bases, in_bases, out_values, in_values, block_layer, in_owner):
        rows, width = gradient.shape[1:]
        blk = out_bases.shape[1]
        jn = width // blk
        slots = yn * ZN
        bf16, f32 = jnp.bfloat16, jnp.float32
        any_spec = pl.BlockSpec(memory_space=pl.ANY)
        vmem = pl.BlockSpec(memory_space=pltpu.VMEM)
        dma = pltpu.SemaphoreType.DMA

        def body(*refs):
            kernel(yn, pn, jn, *refs)

        return pl.pallas_call(
            body,
            out_shape=pltpu.VMEM(gradient.shape, bf16),
            in_specs=[any_spec] * 5 + [vmem] * 2,
            out_specs=vmem,
            scratch_shapes=[
                pltpu.SMEM(in_owner.shape, jnp.int32),
                pltpu.SMEM(block_layer.shape, jnp.int32),
                pltpu.VMEM((blk, blk), bf16),
                pltpu.VMEM((blk, blk), bf16),
                pltpu.VMEM((blk, blk), bf16),
                pltpu.VMEM((blk, blk), bf16),
                pltpu.VMEM((blk, blk), f32),
                pltpu.VMEM((slots, rows, blk), bf16),
                pltpu.VMEM((jn, rows, blk), bf16),
                pltpu.VMEM((blk, blk), bf16),
                pltpu.VMEM((blk, blk), bf16),
                pltpu.VMEM((blk, blk), bf16),
                dma((4,)),
                pltpu.SemaphoreType.REGULAR((ZN - 1,)),
                dma((ZN - 1,)),
                dma((ZN - 1,)),
                dma((2, 4, ZN)),
                dma((2, 4, ZN)),
                dma((jn,)),
                dma,
                dma((jn,)),
                dma,
                dma((pn,)),
                dma,
            ],
            compiler_params=pltpu.CompilerParams(
                collective_id=0, has_side_effects=True, vmem_limit_bytes=60 * 1024 * 1024
            ),
        )(in_owner, block_layer, gradient, out_bases, in_bases, out_values, in_values)

    in_specs = (
        P("grad", "dp", None),
        P("grad", None, None),
        P("grad", None, None),
        P("grad", None),
        P(),
        P("grad"),
        P(),
    )
    return jax.shard_map(shards, mesh=mesh, in_specs=in_specs, out_specs=P("grad", "dp", None), check_vma=False)
```

```python
import jax
import jax.numpy as jnp
from jax import lax
from jax.experimental import pallas as pl
from jax.experimental.pallas import tpu as pltpu
from jax.sharding import PartitionSpec as P

DAMPING = 0.1
MESH = pl.DeviceIdType.MESH
ZN = 4
RIGHT, LEFT = 0, 1
UPPER, LOWER = 0, 1
ORDER = (
    ("y", 0, 1, LOWER), ("y", 0, 1, UPPER), ("up", 1, "first"), ("y", 0, 2, LOWER), ("bundle", "down"), ("y", 0, 2, UPPER),
    ("prepare", 0), ("prepare", 1),
    ("z", 1, UPPER), ("up", 1, "rest"), ("up", 2, "all"), ("up", 3, "all"), ("bundle", "up"), ("prepare", 2), ("prepare", 3),

    ("z", 2, UPPER), ("z", 3, UPPER), ("z", 3, LOWER), ("y", 0, 3, LOWER), ("y", 0, 4, LOWER), ("bundle", "far"),
    ("y", 1, 1, UPPER), ("y", 1, 2, UPPER), ("y", 2, 1, UPPER), ("y", 2, 2, UPPER), ("y", 3, 1, UPPER), ("y", 3, 2, UPPER),
    ("y", 3, 1, LOWER), ("y", 3, 2, LOWER),
    ("y", 0, 3, UPPER), ("y", 0, 4, UPPER), ("y", 1, 3, UPPER), ("y", 1, 4, UPPER),
    ("y", 2, 3, UPPER), ("y", 2, 4, UPPER), ("y", 3, 3, UPPER), ("y", 3, 4, UPPER),
    ("owners", UPPER),
    ("z", 1, LOWER), ("z", 2, LOWER), ("bundled", 1), ("bundled", 3), ("y", 3, 3, LOWER), ("y", 3, 4, LOWER),
    ("owners", LOWER), ("project", 0), ("project", 1), ("project", 2), ("project", 3),
)


def owner_device(j):
    return jnp.where(j < 8, 2 * j + 1, jnp.where(j == 8, 0, 10))


def turn(i, p):
    if i < 4:
        n = lax.rem(i + p // 2, 4)
        return jnp.where(n == 0, 0, jnp.where(n == 1, 5, 6 + n))
    n = lax.rem(i - 4 + p // 2, 6)
    return jnp.where(n < 4, n + 1, n + 2)


def owned_block(p):
    return jnp.where(p % 2 == 1, p // 2, jnp.where(p == 0, 8, 9))


def reach(direction, c, h):
    return 4 if ((c == 1) if c in (1, 2) else (h == UPPER)) == (direction == RIGHT) else 3


def eval_where(which, zh):
    return zh % 2 == 0 if which == "first" else zh % 2 == 1 if which == "rest" else True


def dot(a, b, contract):
    return lax.dot_general(a, b, (contract, ((), ())), preferred_element_type=jnp.float32)


def kernel(
    yn, pn, jn,
    owner_in, layer_in, grad_ref, ob_ref, ib_ref, ov_ref, iv_ref,
    out_ref,
    owner_ref, layer_ref, obuf, obt, gbuf, ybuf, rbuf, tall_u, tall_l, tsend_u, tsend_l, tbuf, sbuf, res,
    lsem, zready, zs, zr, bs, br, ys, yr, gs, gr, ts, tr, ms, mr,
):
    g = lax.axis_index("grad")
    p = lax.axis_index("dp")
    y, zh = g // ZN, g % ZN
    rows = grad_ref.shape[1]
    blk = ob_ref.shape[1]
    part = rows // 2
    own_rows = pl.ds(pl.multiple_of(p * rows, rows), rows)
    tall, tsend = (tall_u, tall_l), (tsend_u, tsend_l)

    def half_rows(h):
        return pl.ds(pl.multiple_of(p * rows + h * part, part), part)
    active = (p % 2 == 1) | (p == 0) | (p == 10)
    mine = owned_block(p)

    def remote(src, dst, ssem, rsem, gg, pp):
        return pltpu.make_async_remote_copy(
            src_ref=src, dst_ref=dst, send_sem=ssem, recv_sem=rsem, device_id=(gg, pp), device_id_type=MESH
        )

    def zpeer(k):
        return y * ZN + lax.rem(zh + k + ZN, ZN)

    def ypeer(d):
        return lax.rem(y + d + yn, yn) * ZN + zh

    def slot(d, k):
        return lax.rem(y + d + yn, yn) * ZN + lax.rem(zh - k + ZN, ZN)

    loads = [
        pltpu.make_async_copy(src, dst, lsem.at[i])
        for i, (src, dst) in enumerate(
            (
                (ib_ref.at[0, half_rows(UPPER), :], tall_u.at[g]), (ib_ref.at[0, half_rows(LOWER), :], tall_l.at[g]),
                (ob_ref.at[0], obuf), (owner_in, owner_ref), (layer_in, layer_ref),
            )
        )
    ]
    for load in loads:
        load.start()

    barrier = pltpu.get_barrier_semaphore()
    for k in (3, 2, 1):
        @pl.when(zh + k < ZN)
        def _():
            pl.semaphore_signal(barrier, inc=1, device_id=(zpeer(k), p), device_id_type=MESH)
    for d in (1, -1, 2, -2):
        pl.semaphore_signal(barrier, inc=1, device_id=(ypeer(d), p), device_id_type=MESH)
    for i in range(1, pn):
        pl.semaphore_signal(barrier, inc=1, device_id=(g, lax.rem(p + i, pn)), device_id_type=MESH)
    pl.semaphore_wait(barrier, pn - 1 + 4 + zh)
    for k in (1, 2, 3):
        @pl.when(zh - k >= 0)
        def _():
            pl.semaphore_signal(zready.at[k - 1], inc=1, device_id=(zpeer(-k), p), device_id_type=MESH)

    for load in loads[:2]:
        load.wait()

    def zcopy(k, h):
        return remote(
            tall[h].at[g], tall[h].at[g], zs.at[k - 1, h], zr.at[k - 1, h], zpeer(k), p
        )

    def zup(k, where=True):
        @pl.when((zh + k < ZN) & where)
        def _():
            pl.semaphore_wait(zready.at[k - 1], 1)
            zcopy(k, UPPER).start()
            zcopy(k, LOWER).start()

    for h in (UPPER, LOWER):
        for k in (1, 3, 2):
            @pl.when(zh + k >= ZN)
            def _():
                zcopy(k, h).start()

    first = jnp.where(zh % 2 == 0, 3, 1)
    kinds = (0, first, 4 - first, 2)

    def ycopy(d, c, here, there, h):
        sign = 1 if d == RIGHT else -1
        piece = tall[h].at[slot(-sign * here, kinds[c])]
        src = piece
        return remote(
            src, piece, ys.at[d, there - 1, c, h], yr.at[d, there - 1, c, h], ypeer(sign * (there - here)), p
        )

    def along(c):
        return (UPPER,) if c in (1, 2) else (UPPER, LOWER)

    def await_piece(sem):
        pltpu.make_async_copy(tall_u.at[0], tall_u.at[0], sem).wait()

    near, far = (2, -2, 1, -1), (4, 3, -3)

    def bundle(k, planes, where):
        @pl.when(where)
        def _():
            for d in planes:
                piece = tall_l.at[slot(d, 0)]
                remote(piece, piece, bs.at[k // 2], br.at[k // 2], zpeer(k), p).start()

    def bundles(which):
        if which == "down":
            bundle(1, near, zh + 1 >= ZN)
            bundle(3, near, zh > 0)
        elif which == "up":
            bundle(1, near, zh + 1 < ZN)
            bundle(3, near, zh == 0)
        else:
            bundle(1, far, zh >= 0)
            bundle(3, far, zh >= 0)

    def bundle_wait(sem):
        size = (len(near) + len(far)) * part
        pltpu.make_async_copy(res.at[pl.ds(0, size), :], res.at[pl.ds(0, size), :], sem).wait()

    def onward(c, here, h):
        for d in (RIGHT, LEFT):
            for there in range(reach(d, c, h), here, -1):
                if here in (0, 2) and there <= here + 2:
                    ycopy(d, c, here, there, h).start()

    def zgot(c, h):
        await_piece(zr.at[kinds[c] - 1, h])
        if h in along(c):
            onward(c, 0, h)

    def ygot(c, here, h):
        for d in (RIGHT, LEFT):
            if here <= reach(d, c, h):
                await_piece(yr.at[d, here - 1, c, h])
        onward(c, here, h)

    onward(0, 0, LOWER)
    onward(0, 0, UPPER)

    def gcopy(i):
        j = turn(i, p)
        return j, remote(
            grad_ref.at[0, :, pl.ds(pl.multiple_of(j * blk, blk), blk)],
            gbuf.at[own_rows, :], gs.at[i], gr, g, owner_device(j),
        )

    for i in range(jn):
        j, copy = gcopy(i)

        @pl.when(owner_device(j) != p)
        def _():
            copy.start()

    @pl.when(active)
    def _():
        pltpu.make_async_copy(
            grad_ref.at[0, :, pl.ds(pl.multiple_of(mine * blk, blk), blk)], gbuf.at[own_rows, :], gr
        ).start()

    for load in loads[2:]:
        load.wait()
    layer = layer_ref[0]

    def prepare(n):
        part = slice(n * (blk // 4), (n + 1) * (blk // 4))

        @pl.when(active)
        def _():
            obt[:, part] = obuf[part, :].T
            spread = jnp.broadcast_to(ov_ref[...], (blk // 4, blk)).T
            values = iv_ref[:, pl.ds(pl.multiple_of(mine * blk + n * (blk // 4), blk // 4), blk // 4)]
            values = jnp.where(layer == 0, values[0:1], values[1:2])
            rbuf[:, part] = 1.0 / (spread * values + DAMPING)

    def project(n):
        lo, size = n * (blk // 4), blk // 4

        @pl.when(active)
        def _():
            if lo == 0:
                pltpu.make_async_copy(gbuf, gbuf, gr).wait()
            ybuf[lo : lo + size, :] = dot(obt[lo : lo + size, :], gbuf[...], ((1,), (0,))).astype(jnp.bfloat16)

    def tcopy(i, h):
        j = turn(i, p)
        return j, remote(tsend[h].at[j], tbuf.at[half_rows(h), :], ts.at[i, h], tr, g, owner_device(j))

    def owners(h):
        for i in range(jn):
            j, copy = tcopy(i, h)
            tsend[h][j] = tall[h][owner_ref[layer, j]]

            @pl.when(owner_device(j) != p)
            def _():
                copy.start()

        @pl.when(active)
        def _():
            pltpu.make_async_copy(tsend[h].at[mine], tbuf.at[half_rows(h), :], tr).start()

    for step in ORDER:
        what, n = step[0], step[1]
        if what == "up":
            zup(n, eval_where(step[2], zh))
        elif what == "z":
            zgot(n, step[2])
        elif what == "y":
            ygot(n, step[2], step[3])
        elif what == "bundle":
            bundles(n)
        elif what == "bundled":
            bundle_wait(br.at[n // 2])
        elif what == "prepare":
            prepare(n)
        elif what == "project":
            project(n)
        else:
            owners(n)

    def mcopy(dest):
        strip = pl.ds(pl.multiple_of(dest * rows, rows), rows)
        cols = pl.ds(pl.multiple_of(mine * blk, blk), blk)
        return res.at[strip, :], out_ref.at[0, :, cols]

    half = blk // 2
    parts = 2
    size, targets = blk // parts, pn // parts

    @pl.when(active)
    def _():
        pltpu.make_async_copy(tbuf, tbuf, tr).wait()
        for lo in (0, half):
            moments = dot(ybuf[lo : lo + half, :], tbuf[...], ((1,), (0,)))
            sbuf[lo : lo + half, :] = (moments * rbuf[lo : lo + half, :]).astype(jnp.bfloat16)
        for n in range(parts):
            turn = lax.rem(n + (p // 4 + 2) // (4 // parts), parts)
            part = pl.ds(pl.multiple_of(turn * size, size), size)
            mixed = dot(obuf[part, :], sbuf[...], ((1,), (0,))).astype(jnp.bfloat16)
            res[part, :] = dot(mixed, tbuf[...], ((1,), (1,))).astype(jnp.bfloat16)
            for i in sorted(range(targets), key=lambda i: i // 2 % 2):
                dest = turn * targets + i + 2 * (1 - p // 2 % 2) - 4 * (i // 2 % 2) * (1 - p // 2 % 2)
                src, dst = mcopy(dest)

                @pl.when(dest != p)
                def _():
                    remote(src, dst, ms.at[dest], mr, g, dest).start()

                @pl.when(dest == p)
                def _():
                    pltpu.make_async_copy(src, dst, mr).start()

    pltpu.make_async_copy(out_ref.at[0], out_ref.at[0], mr).wait()

    for h in (UPPER, LOWER):
        for k in (1, 2, 3):
            await_piece(zs.at[k - 1, h])
        for c in range(ZN):
            for d in (RIGHT, LEFT):
                for there in range(1, reach(d, c, h) + 1):
                    if h in along(c):
                        await_piece(ys.at[d, there - 1, c, h])
    for k in (1, 3):
        bundle_wait(bs.at[k // 2])
    for i in range(jn):
        j, copy = gcopy(i)

        @pl.when(owner_device(j) != p)
        def _():
            copy.wait_send()
            for h in (UPPER, LOWER):
                await_piece(ts.at[i, h])

    @pl.when(active)
    def _():
        for i in range(pn):
            src, dst = mcopy(i)

            @pl.when(i != p)
            def _():
                remote(src, dst, ms.at[i], mr, g, i).wait_send()


def solution(mesh):
    yn = mesh.shape["grad"] // ZN
    pn = mesh.shape["dp"]

    def shards(gradient, out_bases, in_bases, out_values, in_values, block_layer, in_owner):
        rows, width = gradient.shape[1:]
        blk = out_bases.shape[1]
        jn = width // blk
        slots = yn * ZN
        bf16, f32 = jnp.bfloat16, jnp.float32
        any_spec = pl.BlockSpec(memory_space=pl.ANY)
        vmem = pl.BlockSpec(memory_space=pltpu.VMEM)
        dma = pltpu.SemaphoreType.DMA

        def body(*refs):
            kernel(yn, pn, jn, *refs)

        return pl.pallas_call(
            body,
            out_shape=pltpu.VMEM(gradient.shape, bf16),
            in_specs=[any_spec] * 5 + [vmem] * 2,
            out_specs=vmem,
            scratch_shapes=[
                pltpu.SMEM(in_owner.shape, jnp.int32),
                pltpu.SMEM(block_layer.shape, jnp.int32),
                pltpu.VMEM((blk, blk), bf16),
                pltpu.VMEM((blk, blk), bf16),
                pltpu.VMEM((blk, blk), bf16),
                pltpu.VMEM((blk, blk), bf16),
                pltpu.VMEM((blk, blk), f32),
                pltpu.VMEM((slots, rows // 2, blk), bf16),
                pltpu.VMEM((slots, rows // 2, blk), bf16),
                pltpu.VMEM((jn, rows // 2, blk), bf16),
                pltpu.VMEM((jn, rows // 2, blk), bf16),
                pltpu.VMEM((blk, blk), bf16),
                pltpu.VMEM((blk, blk), bf16),
                pltpu.VMEM((blk, blk), bf16),
                dma((5,)),
                pltpu.SemaphoreType.REGULAR((ZN - 1,)),
                dma((ZN - 1, 2)),
                dma((ZN - 1, 2)),
                dma((2,)),
                dma((2,)),
                dma((2, 4, ZN, 2)),
                dma((2, 4, ZN, 2)),
                dma((jn,)),
                dma,
                dma((jn, 2)),
                dma,
                dma((pn,)),
                dma,
            ],
            compiler_params=pltpu.CompilerParams(
                collective_id=0, has_side_effects=True, vmem_limit_bytes=60 * 1024 * 1024
            ),
        )(in_owner, block_layer, gradient, out_bases, in_bases, out_values, in_values)

    in_specs = (
        P("grad", "dp", None),
        P("grad", None, None),
        P("grad", None, None),
        P("grad", None),
        P(),
        P("grad"),
        P(),
    )
    return jax.shard_map(shards, mesh=mesh, in_specs=in_specs, out_specs=P("grad", "dp", None), check_vma=False)
```

```python
import jax
import jax.numpy as jnp
from jax import lax
from jax.experimental import pallas as pl
from jax.experimental.pallas import tpu as pltpu
from jax.sharding import PartitionSpec as P

DAMPING = 0.1
MESH = pl.DeviceIdType.MESH
ZN = 4
RIGHT, LEFT = 0, 1
UPPER, LOWER = 0, 1
ORDER = (
    ("y", 0, 1, LOWER), ("y", 0, 1, UPPER), ("up", 1, "first"), ("y", 0, 2, LOWER), ("bundle", "down"), ("y", 0, 2, UPPER),
    ("prepare", 0), ("prepare", 1),
    ("z", 1, UPPER), ("up", 1, "rest"), ("up", 2, "all"), ("up", 3, "all"), ("bundle", "up"), ("prepare", 2), ("prepare", 3),

    ("z", 2, UPPER), ("z", 3, UPPER), ("z", 3, LOWER), ("y", 0, 3, LOWER), ("y", 0, 4, LOWER), ("bundle", "far"),
    ("y", 1, 1, UPPER), ("y", 1, 2, UPPER), ("y", 2, 1, UPPER), ("y", 2, 2, UPPER), ("y", 3, 1, UPPER), ("y", 3, 2, UPPER),
    ("y", 3, 1, LOWER), ("y", 3, 2, LOWER),
    ("y", 0, 3, UPPER), ("y", 0, 4, UPPER), ("y", 1, 3, UPPER), ("y", 1, 4, UPPER),
    ("y", 2, 3, UPPER), ("y", 2, 4, UPPER), ("y", 3, 3, UPPER), ("y", 3, 4, UPPER),
    ("owners", UPPER),
    ("z", 1, LOWER), ("z", 2, LOWER), ("bundled", 1), ("bundled", 3), ("y", 3, 3, LOWER), ("y", 3, 4, LOWER),
    ("owners", LOWER), ("project", 0), ("project", 1), ("project", 2), ("project", 3),
)


def owner_device(j):
    return jnp.where(j < 8, 2 * j + 1, jnp.where(j == 8, 0, 10))


def turn(i, p):
    if i < 4:
        n = lax.rem(i + p // 2, 4)
        return jnp.where(n == 0, 0, jnp.where(n == 1, 5, 6 + n))
    n = lax.rem(i - 4 + p // 2, 6)
    return jnp.where(n < 4, n + 1, n + 2)


def owned_block(p):
    return jnp.where(p % 2 == 1, p // 2, jnp.where(p == 0, 8, 9))


def reach(direction, c, h):
    return 4 if ((c == 1) if c in (1, 2) else (h == UPPER)) == (direction == RIGHT) else 3


def eval_where(which, zh):
    return zh % 2 == 0 if which == "first" else zh % 2 == 1 if which == "rest" else True


def dot(a, b, contract):
    return lax.dot_general(a, b, (contract, ((), ())), preferred_element_type=jnp.float32)


def kernel(
    yn, pn, jn,
    owner_in, layer_in, grad_ref, ob_ref, ib_ref, ov_in, iv_in,
    out_ref,
    owner_ref, layer_ref, ov_ref, iv_ref, obuf, obt, gbuf, ybuf, rbuf, tall_u, tall_l, tsend_u, tsend_l, tbuf, sbuf, res,
    lsem, zready, zs, zr, bs, br, ys, yr, gs, gr, ts, tr, ms, mr,
):
    g = lax.axis_index("grad")
    p = lax.axis_index("dp")
    y, zh = g // ZN, g % ZN
    rows = grad_ref.shape[1]
    blk = ob_ref.shape[1]
    part = rows // 2
    own_rows = pl.ds(pl.multiple_of(p * rows, rows), rows)
    tall, tsend = (tall_u, tall_l), (tsend_u, tsend_l)

    def half_rows(h):
        return pl.ds(pl.multiple_of(p * rows + h * part, part), part)
    active = (p % 2 == 1) | (p == 0) | (p == 10)
    mine = owned_block(p)

    def remote(src, dst, ssem, rsem, gg, pp):
        return pltpu.make_async_remote_copy(
            src_ref=src, dst_ref=dst, send_sem=ssem, recv_sem=rsem, device_id=(gg, pp), device_id_type=MESH
        )

    def zpeer(k):
        return y * ZN + lax.rem(zh + k + ZN, ZN)

    def ypeer(d):
        return lax.rem(y + d + yn, yn) * ZN + zh

    def slot(d, k):
        return lax.rem(y + d + yn, yn) * ZN + lax.rem(zh - k + ZN, ZN)

    loads = [
        pltpu.make_async_copy(src, dst, lsem.at[i])
        for i, (src, dst) in enumerate(
            (
                (ib_ref.at[0, half_rows(UPPER), :], tall_u.at[g]), (ib_ref.at[0, half_rows(LOWER), :], tall_l.at[g]),
                (ob_ref.at[0], obuf), (owner_in, owner_ref), (layer_in, layer_ref),
                (ov_in, ov_ref), (iv_in, iv_ref),
            )
        )
    ]
    for load in loads:
        load.start()

    barrier = pltpu.get_barrier_semaphore()
    for k in (3, 2, 1):
        @pl.when(zh + k < ZN)
        def _():
            pl.semaphore_signal(barrier, inc=1, device_id=(zpeer(k), p), device_id_type=MESH)
    for d in (1, -1, 2, -2):
        pl.semaphore_signal(barrier, inc=1, device_id=(ypeer(d), p), device_id_type=MESH)
    for i in range(1, pn):
        pl.semaphore_signal(barrier, inc=1, device_id=(g, lax.rem(p + i, pn)), device_id_type=MESH)
    pl.semaphore_wait(barrier, pn - 1 + 4 + zh)
    for k in (1, 2, 3):
        @pl.when(zh - k >= 0)
        def _():
            pl.semaphore_signal(zready.at[k - 1], inc=1, device_id=(zpeer(-k), p), device_id_type=MESH)

    for load in loads[:2]:
        load.wait()

    def zcopy(k, h):
        return remote(
            tall[h].at[g], tall[h].at[g], zs.at[k - 1, h], zr.at[k - 1, h], zpeer(k), p
        )

    def zup(k, where=True):
        @pl.when((zh + k < ZN) & where)
        def _():
            pl.semaphore_wait(zready.at[k - 1], 1)
            zcopy(k, UPPER).start()
            zcopy(k, LOWER).start()

    for h in (UPPER, LOWER):
        for k in (1, 3, 2):
            @pl.when(zh + k >= ZN)
            def _():
                zcopy(k, h).start()

    first = jnp.where(zh % 2 == 0, 3, 1)
    kinds = (0, first, 4 - first, 2)

    def ycopy(d, c, here, there, h):
        sign = 1 if d == RIGHT else -1
        piece = tall[h].at[slot(-sign * here, kinds[c])]
        src = piece
        return remote(
            src, piece, ys.at[d, there - 1, c, h], yr.at[d, there - 1, c, h], ypeer(sign * (there - here)), p
        )

    def along(c):
        return (UPPER,) if c in (1, 2) else (UPPER, LOWER)

    def await_piece(sem):
        pltpu.make_async_copy(tall_u.at[0], tall_u.at[0], sem).wait()

    near, far = (2, -2, 1, -1), (4, 3, -3)

    def bundle(k, planes, where):
        @pl.when(where)
        def _():
            for d in planes:
                piece = tall_l.at[slot(d, 0)]
                remote(piece, piece, bs.at[k // 2], br.at[k // 2], zpeer(k), p).start()

    def bundles(which):
        if which == "down":
            bundle(1, near, zh + 1 >= ZN)
            bundle(3, near, zh > 0)
        elif which == "up":
            bundle(1, near, zh + 1 < ZN)
            bundle(3, near, zh == 0)
        else:
            bundle(1, far, zh >= 0)
            bundle(3, far, zh >= 0)

    def bundle_wait(sem):
        size = (len(near) + len(far)) * part
        pltpu.make_async_copy(res.at[pl.ds(0, size), :], res.at[pl.ds(0, size), :], sem).wait()

    def onward(c, here, h):
        for d in (RIGHT, LEFT):
            for there in range(reach(d, c, h), here, -1):
                if here in (0, 2) and there <= here + 2:
                    ycopy(d, c, here, there, h).start()

    def zgot(c, h):
        await_piece(zr.at[kinds[c] - 1, h])
        if h in along(c):
            onward(c, 0, h)

    def ygot(c, here, h):
        for d in (RIGHT, LEFT):
            if here <= reach(d, c, h):
                await_piece(yr.at[d, here - 1, c, h])
        onward(c, here, h)

    onward(0, 0, LOWER)
    onward(0, 0, UPPER)

    def gcopy(i):
        j = turn(i, p)
        return j, remote(
            grad_ref.at[0, :, pl.ds(pl.multiple_of(j * blk, blk), blk)],
            gbuf.at[own_rows, :], gs.at[i], gr, g, owner_device(j),
        )

    for i in range(jn):
        j, copy = gcopy(i)

        @pl.when(owner_device(j) != p)
        def _():
            copy.start()

    @pl.when(active)
    def _():
        pltpu.make_async_copy(
            grad_ref.at[0, :, pl.ds(pl.multiple_of(mine * blk, blk), blk)], gbuf.at[own_rows, :], gr
        ).start()

    for load in loads[2:]:
        load.wait()
    layer = layer_ref[0]

    def prepare(n):
        part = slice(n * (blk // 4), (n + 1) * (blk // 4))

        @pl.when(active)
        def _():
            obt[:, part] = obuf[part, :].T
            spread = jnp.broadcast_to(ov_ref[...], (blk // 4, blk)).T
            values = iv_ref[:, pl.ds(pl.multiple_of(mine * blk + n * (blk // 4), blk // 4), blk // 4)]
            values = jnp.where(layer == 0, values[0:1], values[1:2])
            rbuf[:, part] = 1.0 / (spread * values + DAMPING)

    def project(n):
        lo, size = n * (blk // 4), blk // 4

        @pl.when(active)
        def _():
            if lo == 0:
                pltpu.make_async_copy(gbuf, gbuf, gr).wait()
            ybuf[lo : lo + size, :] = dot(obt[lo : lo + size, :], gbuf[...], ((1,), (0,))).astype(jnp.bfloat16)

    def tcopy(i, h):
        j = turn(i, p)
        return j, remote(tsend[h].at[j], tbuf.at[half_rows(h), :], ts.at[i, h], tr, g, owner_device(j))

    def owners(h):
        for i in range(jn):
            j, copy = tcopy(i, h)
            tsend[h][j] = tall[h][owner_ref[layer, j]]

            @pl.when(owner_device(j) != p)
            def _():
                copy.start()

        @pl.when(active)
        def _():
            pltpu.make_async_copy(tsend[h].at[mine], tbuf.at[half_rows(h), :], tr).start()

    for step in ORDER:
        what, n = step[0], step[1]
        if what == "up":
            zup(n, eval_where(step[2], zh))
        elif what == "z":
            zgot(n, step[2])
        elif what == "y":
            ygot(n, step[2], step[3])
        elif what == "bundle":
            bundles(n)
        elif what == "bundled":
            bundle_wait(br.at[n // 2])
        elif what == "prepare":
            prepare(n)
        elif what == "project":
            project(n)
        else:
            owners(n)

    def mcopy(dest):
        strip = pl.ds(pl.multiple_of(dest * rows, rows), rows)
        cols = pl.ds(pl.multiple_of(mine * blk, blk), blk)
        return res.at[strip, :], out_ref.at[0, :, cols]

    half = blk // 2
    parts = 2
    size, targets = blk // parts, pn // parts

    @pl.when(active)
    def _():
        pltpu.make_async_copy(tbuf, tbuf, tr).wait()
        for lo in (0, half):
            moments = dot(ybuf[lo : lo + half, :], tbuf[...], ((1,), (0,)))
            sbuf[lo : lo + half, :] = (moments * rbuf[lo : lo + half, :]).astype(jnp.bfloat16)
        for n in range(parts):
            turn = lax.rem(n + (p // 4 + 2) // (4 // parts), parts)
            part = pl.ds(pl.multiple_of(turn * size, size), size)
            mixed = dot(obuf[part, :], sbuf[...], ((1,), (0,))).astype(jnp.bfloat16)
            res[part, :] = dot(mixed, tbuf[...], ((1,), (1,))).astype(jnp.bfloat16)
            for i in sorted(range(targets), key=lambda i: i // 2 % 2):
                dest = turn * targets + i + 2 * (1 - p // 2 % 2) - 4 * (i // 2 % 2) * (1 - p // 2 % 2)
                src, dst = mcopy(dest)

                @pl.when(dest != p)
                def _():
                    remote(src, dst, ms.at[dest], mr, g, dest).start()

                @pl.when(dest == p)
                def _():
                    pltpu.make_async_copy(src, dst, mr).start()

    pltpu.make_async_copy(out_ref.at[0], out_ref.at[0], mr).wait()

    for h in (UPPER, LOWER):
        for k in (1, 2, 3):
            await_piece(zs.at[k - 1, h])
        for c in range(ZN):
            for d in (RIGHT, LEFT):
                for there in range(1, reach(d, c, h) + 1):
                    if h in along(c):
                        await_piece(ys.at[d, there - 1, c, h])
    for k in (1, 3):
        bundle_wait(bs.at[k // 2])
    for i in range(jn):
        j, copy = gcopy(i)

        @pl.when(owner_device(j) != p)
        def _():
            copy.wait_send()
            for h in (UPPER, LOWER):
                await_piece(ts.at[i, h])

    @pl.when(active)
    def _():
        for i in range(pn):
            src, dst = mcopy(i)

            @pl.when(i != p)
            def _():
                remote(src, dst, ms.at[i], mr, g, i).wait_send()


def solution(mesh):
    yn = mesh.shape["grad"] // ZN
    pn = mesh.shape["dp"]

    def shards(gradient, out_bases, in_bases, out_values, in_values, block_layer, in_owner):
        rows, width = gradient.shape[1:]
        blk = out_bases.shape[1]
        jn = width // blk
        slots = yn * ZN
        bf16, f32 = jnp.bfloat16, jnp.float32
        any_spec = pl.BlockSpec(memory_space=pl.ANY)
        vmem = pl.BlockSpec(memory_space=pltpu.VMEM)
        dma = pltpu.SemaphoreType.DMA

        def body(*refs):
            kernel(yn, pn, jn, *refs)

        return pl.pallas_call(
            body,
            out_shape=pltpu.VMEM(gradient.shape, bf16),
            in_specs=[any_spec] * 7,
            out_specs=vmem,
            scratch_shapes=[
                pltpu.SMEM(in_owner.shape, jnp.int32),
                pltpu.SMEM(block_layer.shape, jnp.int32),
                pltpu.VMEM(out_values.shape, f32),
                pltpu.VMEM(in_values.shape, f32),
                pltpu.VMEM((blk, blk), bf16),
                pltpu.VMEM((blk, blk), bf16),
                pltpu.VMEM((blk, blk), bf16),
                pltpu.VMEM((blk, blk), bf16),
                pltpu.VMEM((blk, blk), f32),
                pltpu.VMEM((slots, rows // 2, blk), bf16),
                pltpu.VMEM((slots, rows // 2, blk), bf16),
                pltpu.VMEM((jn, rows // 2, blk), bf16),
                pltpu.VMEM((jn, rows // 2, blk), bf16),
                pltpu.VMEM((blk, blk), bf16),
                pltpu.VMEM((blk, blk), bf16),
                pltpu.VMEM((blk, blk), bf16),
                dma((7,)),
                pltpu.SemaphoreType.REGULAR((ZN - 1,)),
                dma((ZN - 1, 2)),
                dma((ZN - 1, 2)),
                dma((2,)),
                dma((2,)),
                dma((2, 4, ZN, 2)),
                dma((2, 4, ZN, 2)),
                dma((jn,)),
                dma,
                dma((jn, 2)),
                dma,
                dma((pn,)),
                dma,
            ],
            compiler_params=pltpu.CompilerParams(
                collective_id=0, has_side_effects=True, vmem_limit_bytes=60 * 1024 * 1024
            ),
        )(in_owner, block_layer, gradient, out_bases, in_bases, out_values, in_values)

    in_specs = (
        P("grad", "dp", None),
        P("grad", None, None),
        P("grad", None, None),
        P("grad", None),
        P(),
        P("grad"),
        P(),
    )
    return jax.shard_map(shards, mesh=mesh, in_specs=in_specs, out_specs=P("grad", "dp", None), check_vma=False)
```

```python
import jax
import jax.numpy as jnp
from jax import lax
from jax.experimental import pallas as pl
from jax.experimental.pallas import tpu as pltpu
from jax.sharding import PartitionSpec as P

DAMPING = 0.1
MESH = pl.DeviceIdType.MESH
ZN = 4
RIGHT, LEFT = 0, 1
UPPER, LOWER = 0, 1
ORDER = (
    ("y", 0, 1, LOWER), ("y", 0, 1, UPPER), ("up", 1, "first"), ("y", 0, 2, LOWER), ("bundle", "down"), ("y", 0, 2, UPPER),
    ("prepare", 0), ("prepare", 1),
    ("z", 1, UPPER), ("up", 1, "rest"), ("up", 2, "all"), ("up", 3, "all"), ("bundle", "up"), ("prepare", 2), ("prepare", 3),

    ("z", 2, UPPER), ("z", 3, UPPER), ("z", 3, LOWER), ("y", 0, 3, LOWER), ("y", 0, 4, LOWER), ("bundle", "far"),
    ("y", 1, 1, UPPER), ("y", 1, 2, UPPER), ("y", 2, 1, UPPER), ("y", 2, 2, UPPER), ("y", 3, 1, UPPER), ("y", 3, 2, UPPER),
    ("y", 3, 1, LOWER), ("y", 3, 2, LOWER),
    ("y", 0, 3, UPPER), ("y", 0, 4, UPPER), ("y", 1, 3, UPPER), ("y", 1, 4, UPPER),
    ("y", 2, 3, UPPER), ("y", 2, 4, UPPER), ("y", 3, 3, UPPER), ("y", 3, 4, UPPER),
    ("owners", UPPER),
    ("z", 1, LOWER), ("z", 2, LOWER), ("bundled", 1), ("bundled", 3), ("y", 3, 3, LOWER), ("y", 3, 4, LOWER),
    ("owners", LOWER), ("project", 0), ("project", 1), ("project", 2), ("project", 3),
)


def owner_device(j):
    return jnp.where(j < 8, 2 * j + 1, jnp.where(j == 8, 0, 10))


def turn(i, p):
    if i < 4:
        n = lax.rem(i + p // 2, 4)
        return jnp.where(n == 0, 0, jnp.where(n == 1, 5, 6 + n))
    n = lax.rem(i - 4 + p // 2, 6)
    return jnp.where(n < 4, n + 1, n + 2)


def owned_block(p):
    return jnp.where(p % 2 == 1, p // 2, jnp.where(p == 0, 8, 9))


def reach(direction, c, h):
    return 4 if ((c == 1) if c in (1, 2) else (h == UPPER)) == (direction == RIGHT) else 3


def eval_where(which, zh):
    return zh % 2 == 0 if which == "first" else zh % 2 == 1 if which == "rest" else True


def dot(a, b, contract):
    return lax.dot_general(a, b, (contract, ((), ())), preferred_element_type=jnp.float32)


def kernel(
    yn, pn, jn,
    owner_in, layer_in, grad_ref, ob_ref, ib_ref, ov_in, iv_in,
    out_ref,
    owner_ref, layer_ref, ov_ref, iv_ref, obuf, obt, gbuf, ybuf, rbuf, xbuf, tall_u, tall_l, tsend_u, tsend_l, tbuf, sbuf, res,
    lsem, zready, zs, zr, bs, br, ys, yr, gs, gr, ts, tr, ms, mr,
):
    g = lax.axis_index("grad")
    p = lax.axis_index("dp")
    y, zh = g // ZN, g % ZN
    rows = grad_ref.shape[1]
    blk = ob_ref.shape[1]
    part = rows // 2
    own_rows = pl.ds(pl.multiple_of(p * rows, rows), rows)
    tall, tsend = (tall_u, tall_l), (tsend_u, tsend_l)

    def half_rows(h):
        return pl.ds(pl.multiple_of(h * (blk // 2) + p * part, part), part)
    active = (p % 2 == 1) | (p == 0) | (p == 10)
    mine = owned_block(p)

    def remote(src, dst, ssem, rsem, gg, pp):
        return pltpu.make_async_remote_copy(
            src_ref=src, dst_ref=dst, send_sem=ssem, recv_sem=rsem, device_id=(gg, pp), device_id_type=MESH
        )

    def zpeer(k):
        return y * ZN + lax.rem(zh + k + ZN, ZN)

    def ypeer(d):
        return lax.rem(y + d + yn, yn) * ZN + zh

    def slot(d, k):
        return lax.rem(y + d + yn, yn) * ZN + lax.rem(zh - k + ZN, ZN)

    loads = [
        pltpu.make_async_copy(src, dst, lsem.at[i])
        for i, (src, dst) in enumerate(
            (
                (ib_ref.at[0, half_rows(UPPER), :], tall_u.at[g]), (ib_ref.at[0, half_rows(LOWER), :], tall_l.at[g]),
                (ob_ref.at[0], obuf), (owner_in, owner_ref), (layer_in, layer_ref),
                (ov_in, ov_ref), (iv_in, iv_ref),
            )
        )
    ]
    for load in loads:
        load.start()

    barrier = pltpu.get_barrier_semaphore()
    for k in (3, 2, 1):
        @pl.when(zh + k < ZN)
        def _():
            pl.semaphore_signal(barrier, inc=1, device_id=(zpeer(k), p), device_id_type=MESH)
    for d in (1, -1, 2, -2):
        pl.semaphore_signal(barrier, inc=1, device_id=(ypeer(d), p), device_id_type=MESH)
    for i in range(1, pn):
        pl.semaphore_signal(barrier, inc=1, device_id=(g, lax.rem(p + i, pn)), device_id_type=MESH)
    pl.semaphore_wait(barrier, pn - 1 + 4 + zh)
    for k in (1, 2, 3):
        @pl.when(zh - k >= 0)
        def _():
            pl.semaphore_signal(zready.at[k - 1], inc=1, device_id=(zpeer(-k), p), device_id_type=MESH)

    for load in loads[:2]:
        load.wait()

    def zcopy(k, h):
        return remote(
            tall[h].at[g], tall[h].at[g], zs.at[k - 1, h], zr.at[k - 1, h], zpeer(k), p
        )

    def zup(k, where=True):
        @pl.when((zh + k < ZN) & where)
        def _():
            pl.semaphore_wait(zready.at[k - 1], 1)
            zcopy(k, UPPER).start()
            zcopy(k, LOWER).start()

    for h in (UPPER, LOWER):
        for k in (1, 3, 2):
            @pl.when(zh + k >= ZN)
            def _():
                zcopy(k, h).start()

    first = jnp.where(zh % 2 == 0, 3, 1)
    kinds = (0, first, 4 - first, 2)

    def ycopy(d, c, here, there, h):
        sign = 1 if d == RIGHT else -1
        piece = tall[h].at[slot(-sign * here, kinds[c])]
        src = piece
        return remote(
            src, piece, ys.at[d, there - 1, c, h], yr.at[d, there - 1, c, h], ypeer(sign * (there - here)), p
        )

    def along(c):
        return (UPPER,) if c in (1, 2) else (UPPER, LOWER)

    def await_piece(sem):
        pltpu.make_async_copy(tall_u.at[0], tall_u.at[0], sem).wait()

    near, far = (2, -2, 1, -1), (4, 3, -3)

    def bundle(k, planes, where):
        @pl.when(where)
        def _():
            for d in planes:
                piece = tall_l.at[slot(d, 0)]
                remote(piece, piece, bs.at[k // 2], br.at[k // 2], zpeer(k), p).start()

    def bundles(which):
        if which == "down":
            bundle(1, near, zh + 1 >= ZN)
            bundle(3, near, zh > 0)
        elif which == "up":
            bundle(1, near, zh + 1 < ZN)
            bundle(3, near, zh == 0)
        else:
            bundle(1, far, zh >= 0)
            bundle(3, far, zh >= 0)

    def bundle_wait(sem):
        size = (len(near) + len(far)) * part
        pltpu.make_async_copy(res.at[pl.ds(0, size), :], res.at[pl.ds(0, size), :], sem).wait()

    def onward(c, here, h):
        for d in (RIGHT, LEFT):
            for there in range(reach(d, c, h), here, -1):
                if here in (0, 2) and there <= here + 2:
                    ycopy(d, c, here, there, h).start()

    def zgot(c, h):
        await_piece(zr.at[kinds[c] - 1, h])
        if h in along(c):
            onward(c, 0, h)

    def ygot(c, here, h):
        for d in (RIGHT, LEFT):
            if here <= reach(d, c, h):
                await_piece(yr.at[d, here - 1, c, h])
        onward(c, here, h)

    onward(0, 0, LOWER)
    onward(0, 0, UPPER)

    def gcopy(i):
        j = turn(i, p)
        return j, remote(
            grad_ref.at[0, :, pl.ds(pl.multiple_of(j * blk, blk), blk)],
            gbuf.at[own_rows, :], gs.at[i], gr, g, owner_device(j),
        )

    for i in range(jn):
        j, copy = gcopy(i)

        @pl.when(owner_device(j) != p)
        def _():
            copy.start()

    @pl.when(active)
    def _():
        pltpu.make_async_copy(
            grad_ref.at[0, :, pl.ds(pl.multiple_of(mine * blk, blk), blk)], gbuf.at[own_rows, :], gr
        ).start()

    for load in loads[2:]:
        load.wait()
    layer = layer_ref[0]

    def prepare(n):
        part = slice(n * (blk // 4), (n + 1) * (blk // 4))

        @pl.when(active)
        def _():
            obt[:, part] = obuf[part, :].T
            spread = jnp.broadcast_to(ov_ref[...], (blk // 4, blk)).T
            values = iv_ref[:, pl.ds(pl.multiple_of(mine * blk + n * (blk // 4), blk // 4), blk // 4)]
            values = jnp.where(layer == 0, values[0:1], values[1:2])
            rbuf[:, part] = 1.0 / (spread * values + DAMPING)

    def project(n):
        lo, size = n * (blk // 4), blk // 4

        @pl.when(active)
        def _():
            if lo == 0:
                pltpu.make_async_copy(gbuf, gbuf, gr).wait()
            ybuf[lo : lo + size, :] = dot(obt[lo : lo + size, :], gbuf[...], ((1,), (0,))).astype(jnp.bfloat16)

    def tcopy(i, h):
        j = turn(i, p)
        return j, remote(tsend[h].at[j], tbuf.at[half_rows(h), :], ts.at[i, h], tr.at[h], g, owner_device(j))

    def owners(h):
        for i in range(jn):
            j, copy = tcopy(i, h)
            tsend[h][j] = tall[h][owner_ref[layer, j]]

            @pl.when(owner_device(j) != p)
            def _():
                copy.start()

        @pl.when(active)
        def _():
            pltpu.make_async_copy(tsend[h].at[mine], tbuf.at[half_rows(h), :], tr.at[h]).start()

    for step in ORDER:
        what, n = step[0], step[1]
        if what == "up":
            zup(n, eval_where(step[2], zh))
        elif what == "z":
            zgot(n, step[2])
        elif what == "y":
            ygot(n, step[2], step[3])
        elif what == "bundle":
            bundles(n)
        elif what == "bundled":
            bundle_wait(br.at[n // 2])
        elif what == "prepare":
            prepare(n)
        elif what == "project":
            project(n)
        else:
            owners(n)

    def mcopy(dest):
        strip = pl.ds(pl.multiple_of(dest * rows, rows), rows)
        cols = pl.ds(pl.multiple_of(mine * blk, blk), blk)
        return res.at[strip, :], out_ref.at[0, :, cols]

    half = blk // 2
    parts = 2
    size, targets = blk // parts, pn // parts

    @pl.when(active)
    def _():
        tops = [pl.ds(h * half, half) for h in (UPPER, LOWER)]
        for h in (UPPER, LOWER):
            pltpu.make_async_copy(tbuf.at[tops[h], :], tbuf.at[tops[h], :], tr.at[h]).wait()
            for lo in (0, half):
                some = slice(lo, lo + half)
                product = dot(ybuf[some, tops[h]], tbuf[tops[h], :], ((1,), (0,)))
                if h == UPPER:
                    xbuf[some, :] = product
                else:
                    sbuf[some, :] = ((xbuf[some, :] + product) * rbuf[some, :]).astype(jnp.bfloat16)
        for n in range(parts):
            turn = lax.rem(n + (p // 4 + 2) // (4 // parts), parts)
            part = pl.ds(pl.multiple_of(turn * size, size), size)
            mixed = dot(obuf[part, :], sbuf[...], ((1,), (0,))).astype(jnp.bfloat16)
            res[part, :] = dot(mixed, tbuf[...], ((1,), (1,))).astype(jnp.bfloat16)
            for i in sorted(range(targets), key=lambda i: i // 2 % 2):
                dest = turn * targets + i + 2 * (1 - p // 2 % 2) - 4 * (i // 2 % 2) * (1 - p // 2 % 2)
                src, dst = mcopy(dest)

                @pl.when(dest != p)
                def _():
                    remote(src, dst, ms.at[dest], mr, g, dest).start()

                @pl.when(dest == p)
                def _():
                    pltpu.make_async_copy(src, dst, mr).start()

    pltpu.make_async_copy(out_ref.at[0], out_ref.at[0], mr).wait()

    for h in (UPPER, LOWER):
        for k in (1, 2, 3):
            await_piece(zs.at[k - 1, h])
        for c in range(ZN):
            for d in (RIGHT, LEFT):
                for there in range(1, reach(d, c, h) + 1):
                    if h in along(c):
                        await_piece(ys.at[d, there - 1, c, h])
    for k in (1, 3):
        bundle_wait(bs.at[k // 2])
    for i in range(jn):
        j, copy = gcopy(i)

        @pl.when(owner_device(j) != p)
        def _():
            copy.wait_send()
            for h in (UPPER, LOWER):
                await_piece(ts.at[i, h])

    @pl.when(active)
    def _():
        for i in range(pn):
            src, dst = mcopy(i)

            @pl.when(i != p)
            def _():
                remote(src, dst, ms.at[i], mr, g, i).wait_send()


def solution(mesh):
    yn = mesh.shape["grad"] // ZN
    pn = mesh.shape["dp"]

    def shards(gradient, out_bases, in_bases, out_values, in_values, block_layer, in_owner):
        rows, width = gradient.shape[1:]
        blk = out_bases.shape[1]
        jn = width // blk
        slots = yn * ZN
        bf16, f32 = jnp.bfloat16, jnp.float32
        any_spec = pl.BlockSpec(memory_space=pl.ANY)
        vmem = pl.BlockSpec(memory_space=pltpu.VMEM)
        dma = pltpu.SemaphoreType.DMA

        def body(*refs):
            kernel(yn, pn, jn, *refs)

        return pl.pallas_call(
            body,
            out_shape=pltpu.VMEM(gradient.shape, bf16),
            in_specs=[any_spec] * 7,
            out_specs=vmem,
            scratch_shapes=[
                pltpu.SMEM(in_owner.shape, jnp.int32),
                pltpu.SMEM(block_layer.shape, jnp.int32),
                pltpu.VMEM(out_values.shape, f32),
                pltpu.VMEM(in_values.shape, f32),
                pltpu.VMEM((blk, blk), bf16),
                pltpu.VMEM((blk, blk), bf16),
                pltpu.VMEM((blk, blk), bf16),
                pltpu.VMEM((blk, blk), bf16),
                pltpu.VMEM((blk, blk), f32),
                pltpu.VMEM((blk, blk), f32),
                pltpu.VMEM((slots, rows // 2, blk), bf16),
                pltpu.VMEM((slots, rows // 2, blk), bf16),
                pltpu.VMEM((jn, rows // 2, blk), bf16),
                pltpu.VMEM((jn, rows // 2, blk), bf16),
                pltpu.VMEM((blk, blk), bf16),
                pltpu.VMEM((blk, blk), bf16),
                pltpu.VMEM((blk, blk), bf16),
                dma((7,)),
                pltpu.SemaphoreType.REGULAR((ZN - 1,)),
                dma((ZN - 1, 2)),
                dma((ZN - 1, 2)),
                dma((2,)),
                dma((2,)),
                dma((2, 4, ZN, 2)),
                dma((2, 4, ZN, 2)),
                dma((jn,)),
                dma,
                dma((jn, 2)),
                dma((2,)),
                dma((pn,)),
                dma,
            ],
            compiler_params=pltpu.CompilerParams(
                collective_id=0, has_side_effects=True, vmem_limit_bytes=60 * 1024 * 1024
            ),
        )(in_owner, block_layer, gradient, out_bases, in_bases, out_values, in_values)

    in_specs = (
        P("grad", "dp", None),
        P("grad", None, None),
        P("grad", None, None),
        P("grad", None),
        P(),
        P("grad"),
        P(),
    )
    return jax.shard_map(shards, mesh=mesh, in_specs=in_specs, out_specs=P("grad", "dp", None), check_vma=False)
```

```python
import jax
import jax.numpy as jnp
from jax import lax
from jax.experimental import pallas as pl
from jax.experimental.pallas import tpu as pltpu
from jax.sharding import PartitionSpec as P

DAMPING = 0.1
MESH = pl.DeviceIdType.MESH
ZN = 4
RIGHT, LEFT = 0, 1
UPPER, LOWER = 0, 1
ORDER = (
    ("y", 0, 1, LOWER), ("y", 0, 1, UPPER), ("up", 1, "first"), ("y", 0, 2, LOWER), ("bundle", "down"), ("y", 0, 2, UPPER),
    ("prepare", 0), ("prepare", 1),
    ("z", 1, UPPER), ("up", 1, "rest"), ("up", 2, "all"), ("up", 3, "all"), ("bundle", "up"), ("prepare", 2), ("prepare", 3),

    ("z", 2, UPPER), ("z", 3, UPPER), ("z", 3, LOWER), ("y", 0, 3, LOWER), ("y", 0, 4, LOWER), ("bundle", "far"),
    ("y", 1, 1, UPPER), ("y", 1, 2, UPPER), ("y", 2, 1, UPPER), ("y", 2, 2, UPPER), ("y", 3, 1, UPPER), ("y", 3, 2, UPPER),
    ("y", 3, 1, LOWER), ("y", 3, 2, LOWER),
    ("y", 1, 3, UPPER), ("y", 1, 4, UPPER),
    ("y", 2, 3, UPPER), ("y", 2, 4, UPPER), ("y", 3, 3, UPPER), ("y", 3, 4, UPPER),
    ("y", 0, 3, UPPER), ("y", 0, 4, UPPER), ("owners", UPPER),
    ("z", 1, LOWER), ("z", 2, LOWER), ("bundled", 1), ("bundled", 3), ("y", 3, 3, LOWER), ("y", 3, 4, LOWER),
    ("owners", LOWER), ("project", 0), ("project", 1), ("project", 2), ("project", 3),
)


def owner_device(j):
    return jnp.where(j < 8, 2 * j + 1, jnp.where(j == 8, 0, 10))


def turn(i, p):
    if i < 4:
        n = lax.rem(i + p // 2, 4)
        return jnp.where(n == 0, 0, jnp.where(n == 1, 5, 6 + n))
    n = lax.rem(i - 4 + p // 2, 6)
    return jnp.where(n < 4, n + 1, n + 2)


def owned_block(p):
    return jnp.where(p % 2 == 1, p // 2, jnp.where(p == 0, 8, 9))


def reach(direction, c, h):
    return 4 if ((c == 1) if c in (1, 2) else (h == UPPER)) == (direction == RIGHT) else 3


def eval_where(which, zh):
    return zh % 2 == 0 if which == "first" else zh % 2 == 1 if which == "rest" else True


def dot(a, b, contract):
    return lax.dot_general(a, b, (contract, ((), ())), preferred_element_type=jnp.float32)


def kernel(
    yn, pn, jn,
    owner_in, layer_in, grad_ref, ob_ref, ib_ref, ov_in, iv_in,
    out_ref,
    owner_ref, layer_ref, ov_ref, iv_ref, obuf, obt, gbuf, ybuf, rbuf, xbuf, tall_u, tall_l, tsend_u, tsend_l, tbuf, sbuf, res,
    lsem, zready, zs, zr, bs, br, ys, yr, gs, gr, ts, tr, ms, mr,
):
    g = lax.axis_index("grad")
    p = lax.axis_index("dp")
    y, zh = g // ZN, g % ZN
    rows = grad_ref.shape[1]
    blk = ob_ref.shape[1]
    part = rows // 2
    own_rows = pl.ds(pl.multiple_of(p * rows, rows), rows)
    tall, tsend = (tall_u, tall_l), (tsend_u, tsend_l)

    def half_rows(h):
        return pl.ds(pl.multiple_of(h * (blk // 2) + p * part, part), part)
    active = (p % 2 == 1) | (p == 0) | (p == 10)
    mine = owned_block(p)

    def remote(src, dst, ssem, rsem, gg, pp):
        return pltpu.make_async_remote_copy(
            src_ref=src, dst_ref=dst, send_sem=ssem, recv_sem=rsem, device_id=(gg, pp), device_id_type=MESH
        )

    def zpeer(k):
        return y * ZN + lax.rem(zh + k + ZN, ZN)

    def ypeer(d):
        return lax.rem(y + d + yn, yn) * ZN + zh

    def slot(d, k):
        return lax.rem(y + d + yn, yn) * ZN + lax.rem(zh - k + ZN, ZN)

    loads = [
        pltpu.make_async_copy(src, dst, lsem.at[i])
        for i, (src, dst) in enumerate(
            (
                (ib_ref.at[0, half_rows(UPPER), :], tall_u.at[g]), (ib_ref.at[0, half_rows(LOWER), :], tall_l.at[g]),
                (ob_ref.at[0], obuf), (owner_in, owner_ref), (layer_in, layer_ref),
                (ov_in, ov_ref), (iv_in, iv_ref),
            )
        )
    ]
    for load in loads:
        load.start()

    barrier = pltpu.get_barrier_semaphore()
    for k in (3, 2, 1):
        @pl.when(zh + k < ZN)
        def _():
            pl.semaphore_signal(barrier, inc=1, device_id=(zpeer(k), p), device_id_type=MESH)
    for d in (1, -1, 2, -2):
        pl.semaphore_signal(barrier, inc=1, device_id=(ypeer(d), p), device_id_type=MESH)
    for i in range(1, pn):
        pl.semaphore_signal(barrier, inc=1, device_id=(g, lax.rem(p + i, pn)), device_id_type=MESH)
    pl.semaphore_wait(barrier, pn - 1 + 4 + zh)
    for k in (1, 2, 3):
        @pl.when(zh - k >= 0)
        def _():
            pl.semaphore_signal(zready.at[k - 1], inc=1, device_id=(zpeer(-k), p), device_id_type=MESH)

    for load in loads[:2]:
        load.wait()

    def zcopy(k, h):
        return remote(
            tall[h].at[g], tall[h].at[g], zs.at[k - 1, h], zr.at[k - 1, h], zpeer(k), p
        )

    def zup(k, where=True):
        @pl.when((zh + k < ZN) & where)
        def _():
            pl.semaphore_wait(zready.at[k - 1], 1)
            zcopy(k, UPPER).start()
            zcopy(k, LOWER).start()

    for h in (UPPER, LOWER):
        for k in (1, 3, 2):
            @pl.when(zh + k >= ZN)
            def _():
                zcopy(k, h).start()

    first = jnp.where(zh % 2 == 0, 3, 1)
    kinds = (0, first, 4 - first, 2)

    def ycopy(d, c, here, there, h):
        sign = 1 if d == RIGHT else -1
        piece = tall[h].at[slot(-sign * here, kinds[c])]
        src = piece
        return remote(
            src, piece, ys.at[d, there - 1, c, h], yr.at[d, there - 1, c, h], ypeer(sign * (there - here)), p
        )

    def along(c):
        return (UPPER,) if c in (1, 2) else (UPPER, LOWER)

    def await_piece(sem):
        pltpu.make_async_copy(tall_u.at[0], tall_u.at[0], sem).wait()

    near, far = (2, -2, 1, -1), (4, 3, -3)

    def bundle(k, planes, where):
        @pl.when(where)
        def _():
            for d in planes:
                piece = tall_l.at[slot(d, 0)]
                remote(piece, piece, bs.at[k // 2], br.at[k // 2], zpeer(k), p).start()

    def bundles(which):
        if which == "down":
            bundle(1, near, zh + 1 >= ZN)
            bundle(3, near, zh > 0)
        elif which == "up":
            bundle(1, near, zh + 1 < ZN)
            bundle(3, near, zh == 0)
        else:
            bundle(1, far, zh >= 0)
            bundle(3, far, zh >= 0)

    def bundle_wait(sem):
        size = (len(near) + len(far)) * part
        pltpu.make_async_copy(res.at[pl.ds(0, size), :], res.at[pl.ds(0, size), :], sem).wait()

    def onward(c, here, h):
        for d in (RIGHT, LEFT):
            for there in range(reach(d, c, h), here, -1):
                if here in (0, 2) and there <= here + 2:
                    ycopy(d, c, here, there, h).start()

    def zgot(c, h):
        await_piece(zr.at[kinds[c] - 1, h])
        if h in along(c):
            onward(c, 0, h)

    def ygot(c, here, h):
        for d in (RIGHT, LEFT):
            if here <= reach(d, c, h):
                await_piece(yr.at[d, here - 1, c, h])
        onward(c, here, h)

    onward(0, 0, LOWER)
    onward(0, 0, UPPER)

    def gcopy(i):
        j = turn(i, p)
        return j, remote(
            grad_ref.at[0, :, pl.ds(pl.multiple_of(j * blk, blk), blk)],
            gbuf.at[own_rows, :], gs.at[i], gr, g, owner_device(j),
        )

    for across in (True, False):
        for i in range(jn):
            j, copy = gcopy(i)
            dest = owner_device(j)

            @pl.when((dest != p) & ((dest // 2 % 2 != p // 2 % 2) == across))
            def _():
                copy.start()

    @pl.when(active)
    def _():
        pltpu.make_async_copy(
            grad_ref.at[0, :, pl.ds(pl.multiple_of(mine * blk, blk), blk)], gbuf.at[own_rows, :], gr
        ).start()

    for load in loads[2:]:
        load.wait()
    layer = layer_ref[0]

    def prepare(n):
        part = slice(n * (blk // 4), (n + 1) * (blk // 4))

        @pl.when(active)
        def _():
            obt[:, part] = obuf[part, :].T
            spread = jnp.broadcast_to(ov_ref[...], (blk // 4, blk)).T
            values = iv_ref[:, pl.ds(pl.multiple_of(mine * blk + n * (blk // 4), blk // 4), blk // 4)]
            values = jnp.where(layer == 0, values[0:1], values[1:2])
            rbuf[:, part] = 1.0 / (spread * values + DAMPING)

    def project(n):
        lo, size = n * (blk // 4), blk // 4

        @pl.when(active)
        def _():
            if lo == 0:
                pltpu.make_async_copy(gbuf, gbuf, gr).wait()
            ybuf[lo : lo + size, :] = dot(obt[lo : lo + size, :], gbuf[...], ((1,), (0,))).astype(jnp.bfloat16)

    def tcopy(i, h):
        j = turn(i, p)
        return j, remote(tsend[h].at[j], tbuf.at[half_rows(h), :], ts.at[i, h], tr.at[h], g, owner_device(j))

    def owners(h):
        for i in range(jn):
            j, copy = tcopy(i, h)
            tsend[h][j] = tall[h][owner_ref[layer, j]]

            @pl.when(owner_device(j) != p)
            def _():
                copy.start()

        @pl.when(active)
        def _():
            pltpu.make_async_copy(tsend[h].at[mine], tbuf.at[half_rows(h), :], tr.at[h]).start()

    for step in ORDER:
        what, n = step[0], step[1]
        if what == "up":
            zup(n, eval_where(step[2], zh))
        elif what == "z":
            zgot(n, step[2])
        elif what == "y":
            ygot(n, step[2], step[3])
        elif what == "bundle":
            bundles(n)
        elif what == "bundled":
            bundle_wait(br.at[n // 2])
        elif what == "prepare":
            prepare(n)
        elif what == "project":
            project(n)
        else:
            owners(n)

    def mcopy(dest):
        strip = pl.ds(pl.multiple_of(dest * rows, rows), rows)
        cols = pl.ds(pl.multiple_of(mine * blk, blk), blk)
        return res.at[strip, :], out_ref.at[0, :, cols]

    half = blk // 2
    parts = 2
    size, targets = blk // parts, pn // parts

    @pl.when(active)
    def _():
        tops = [pl.ds(h * half, half) for h in (UPPER, LOWER)]
        for h in (UPPER, LOWER):
            pltpu.make_async_copy(tbuf.at[tops[h], :], tbuf.at[tops[h], :], tr.at[h]).wait()
            for lo in (0, half):
                some = slice(lo, lo + half)
                product = dot(ybuf[some, tops[h]], tbuf[tops[h], :], ((1,), (0,)))
                if h == UPPER:
                    xbuf[some, :] = product
                else:
                    sbuf[some, :] = ((xbuf[some, :] + product) * rbuf[some, :]).astype(jnp.bfloat16)
        for n in range(parts):
            turn = n
            part = pl.ds(pl.multiple_of(turn * size, size), size)
            mixed = dot(obuf[part, :], sbuf[...], ((1,), (0,))).astype(jnp.bfloat16)
            res[part, :] = dot(mixed, tbuf[...], ((1,), (1,))).astype(jnp.bfloat16)
            for i in sorted(range(targets), key=lambda i: i // 2 % 2):
                dest = turn * targets + i + 2 * (1 - p // 2 % 2) - 4 * (i // 2 % 2) * (1 - p // 2 % 2)
                src, dst = mcopy(dest)

                @pl.when(dest != p)
                def _():
                    remote(src, dst, ms.at[dest], mr, g, dest).start()

                @pl.when(dest == p)
                def _():
                    pltpu.make_async_copy(src, dst, mr).start()

    pltpu.make_async_copy(out_ref.at[0], out_ref.at[0], mr).wait()

    for h in (UPPER, LOWER):
        for k in (1, 2, 3):
            await_piece(zs.at[k - 1, h])
        for c in range(ZN):
            for d in (RIGHT, LEFT):
                for there in range(1, reach(d, c, h) + 1):
                    if h in along(c):
                        await_piece(ys.at[d, there - 1, c, h])
    for k in (1, 3):
        bundle_wait(bs.at[k // 2])
    for i in range(jn):
        j, copy = gcopy(i)

        @pl.when(owner_device(j) != p)
        def _():
            copy.wait_send()
            for h in (UPPER, LOWER):
                await_piece(ts.at[i, h])

    @pl.when(active)
    def _():
        for i in range(pn):
            src, dst = mcopy(i)

            @pl.when(i != p)
            def _():
                remote(src, dst, ms.at[i], mr, g, i).wait_send()


def solution(mesh):
    yn = mesh.shape["grad"] // ZN
    pn = mesh.shape["dp"]

    def shards(gradient, out_bases, in_bases, out_values, in_values, block_layer, in_owner):
        rows, width = gradient.shape[1:]
        blk = out_bases.shape[1]
        jn = width // blk
        slots = yn * ZN
        bf16, f32 = jnp.bfloat16, jnp.float32
        any_spec = pl.BlockSpec(memory_space=pl.ANY)
        vmem = pl.BlockSpec(memory_space=pltpu.VMEM)
        dma = pltpu.SemaphoreType.DMA

        def body(*refs):
            kernel(yn, pn, jn, *refs)

        return pl.pallas_call(
            body,
            out_shape=pltpu.VMEM(gradient.shape, bf16),
            in_specs=[any_spec] * 7,
            out_specs=vmem,
            scratch_shapes=[
                pltpu.SMEM(in_owner.shape, jnp.int32),
                pltpu.SMEM(block_layer.shape, jnp.int32),
                pltpu.VMEM(out_values.shape, f32),
                pltpu.VMEM(in_values.shape, f32),
                pltpu.VMEM((blk, blk), bf16),
                pltpu.VMEM((blk, blk), bf16),
                pltpu.VMEM((blk, blk), bf16),
                pltpu.VMEM((blk, blk), bf16),
                pltpu.VMEM((blk, blk), f32),
                pltpu.VMEM((blk, blk), f32),
                pltpu.VMEM((slots, rows // 2, blk), bf16),
                pltpu.VMEM((slots, rows // 2, blk), bf16),
                pltpu.VMEM((jn, rows // 2, blk), bf16),
                pltpu.VMEM((jn, rows // 2, blk), bf16),
                pltpu.VMEM((blk, blk), bf16),
                pltpu.VMEM((blk, blk), bf16),
                pltpu.VMEM((blk, blk), bf16),
                dma((7,)),
                pltpu.SemaphoreType.REGULAR((ZN - 1,)),
                dma((ZN - 1, 2)),
                dma((ZN - 1, 2)),
                dma((2,)),
                dma((2,)),
                dma((2, 4, ZN, 2)),
                dma((2, 4, ZN, 2)),
                dma((jn,)),
                dma,
                dma((jn, 2)),
                dma((2,)),
                dma((pn,)),
                dma,
            ],
            compiler_params=pltpu.CompilerParams(
                collective_id=0, has_side_effects=True, vmem_limit_bytes=60 * 1024 * 1024
            ),
        )(in_owner, block_layer, gradient, out_bases, in_bases, out_values, in_values)

    in_specs = (
        P("grad", "dp", None),
        P("grad", None, None),
        P("grad", None, None),
        P("grad", None),
        P(),
        P("grad"),
        P(),
    )
    return jax.shard_map(shards, mesh=mesh, in_specs=in_specs, out_specs=P("grad", "dp", None), check_vma=False)
```

```python
import jax
import jax.numpy as jnp
from jax import lax
from jax.experimental import pallas as pl
from jax.experimental.pallas import tpu as pltpu
from jax.sharding import PartitionSpec as P

DAMPING = 0.1
MESH = pl.DeviceIdType.MESH
ZN = 4
RIGHT, LEFT = 0, 1
UPPER, LOWER = 0, 1
ORDER = (
    ("y", 0, 1, LOWER), ("y", 0, 1, UPPER), ("up", 1, "first"), ("y", 0, 2, LOWER), ("bundle", "down"), ("y", 0, 2, UPPER),
    ("prepare", 0), ("prepare", 1),
    ("z", 1, UPPER), ("up", 1, "rest"), ("up", 2, "all"), ("up", 3, "all"), ("bundle", "up"), ("prepare", 2), ("prepare", 3),

    ("z", 2, UPPER), ("z", 3, UPPER), ("z", 3, LOWER), ("y", 0, 3, LOWER), ("y", 0, 4, LOWER), ("bundle", "far"),
    ("y", 1, 1, UPPER), ("y", 1, 2, UPPER), ("y", 2, 1, UPPER), ("y", 2, 2, UPPER), ("y", 3, 1, UPPER), ("y", 3, 2, UPPER),
    ("y", 3, 1, LOWER), ("y", 3, 2, LOWER),
    ("y", 0, 3, UPPER), ("y", 0, 4, UPPER), ("y", 1, 3, UPPER), ("y", 1, 4, UPPER),
    ("y", 2, 3, UPPER), ("y", 2, 4, UPPER), ("y", 3, 3, UPPER), ("y", 3, 4, UPPER),
    ("owners", UPPER),
    ("z", 1, LOWER), ("z", 2, LOWER), ("bundled", 1), ("bundled", 3), ("y", 3, 3, LOWER), ("y", 3, 4, LOWER),
    ("owners", LOWER), ("project", 0), ("project", 1), ("project", 2), ("project", 3),
)


def owner_device(j):
    return jnp.where(j < 8, 2 * j + 1, jnp.where(j == 8, 8, 14))


def turn(i, p):
    if i < 4:
        n = lax.rem(i + p // 2, 4)
        return jnp.where(n == 0, 4, jnp.where(n == 1, 7, 6 + n))
    n = lax.rem(i - 4 + p // 2, 6)
    return n + (n >= 4).astype(jnp.int32) + (n >= 6).astype(jnp.int32)


def owned_block(p):
    return jnp.where(p % 2 == 1, p // 2, jnp.where(p == 8, 8, 9))


def reach(direction, c, h):
    return 4 if ((c == 1) if c in (1, 2) else (h == UPPER)) == (direction == RIGHT) else 3


def eval_where(which, zh):
    return zh % 2 == 0 if which == "first" else zh % 2 == 1 if which == "rest" else True


def dot(a, b, contract):
    return lax.dot_general(a, b, (contract, ((), ())), preferred_element_type=jnp.float32)


def kernel(
    yn, pn, jn,
    owner_in, layer_in, grad_ref, ob_ref, ib_ref, ov_in, iv_in,
    out_ref,
    owner_ref, layer_ref, ov_ref, iv_ref, obuf, obt, gbuf, ybuf, rbuf, xbuf, tall_u, tall_l, tsend_u, tsend_l, tbuf, sbuf, res,
    lsem, zready, zs, zr, bs, br, ys, yr, gs, gr, ts, tr, ms, mr,
):
    g = lax.axis_index("grad")
    p = lax.axis_index("dp")
    y, zh = g // ZN, g % ZN
    rows = grad_ref.shape[1]
    blk = ob_ref.shape[1]
    part = rows // 2
    own_rows = pl.ds(pl.multiple_of(p * rows, rows), rows)
    tall, tsend = (tall_u, tall_l), (tsend_u, tsend_l)

    def half_rows(h):
        return pl.ds(pl.multiple_of(h * (blk // 2) + p * part, part), part)
    active = (p % 2 == 1) | (p == 8) | (p == 14)
    mine = owned_block(p)

    def remote(src, dst, ssem, rsem, gg, pp):
        return pltpu.make_async_remote_copy(
            src_ref=src, dst_ref=dst, send_sem=ssem, recv_sem=rsem, device_id=(gg, pp), device_id_type=MESH
        )

    def zpeer(k):
        return y * ZN + lax.rem(zh + k + ZN, ZN)

    def ypeer(d):
        return lax.rem(y + d + yn, yn) * ZN + zh

    def slot(d, k):
        return lax.rem(y + d + yn, yn) * ZN + lax.rem(zh - k + ZN, ZN)

    loads = [
        pltpu.make_async_copy(src, dst, lsem.at[i])
        for i, (src, dst) in enumerate(
            (
                (ib_ref.at[0, half_rows(UPPER), :], tall_u.at[g]), (ib_ref.at[0, half_rows(LOWER), :], tall_l.at[g]),
                (ob_ref.at[0], obuf), (owner_in, owner_ref), (layer_in, layer_ref),
                (ov_in, ov_ref), (iv_in, iv_ref),
            )
        )
    ]
    for load in loads:
        load.start()

    barrier = pltpu.get_barrier_semaphore()
    for k in (3, 2, 1):
        @pl.when(zh + k < ZN)
        def _():
            pl.semaphore_signal(barrier, inc=1, device_id=(zpeer(k), p), device_id_type=MESH)
    for d in (1, -1, 2, -2):
        pl.semaphore_signal(barrier, inc=1, device_id=(ypeer(d), p), device_id_type=MESH)
    for i in range(1, pn):
        pl.semaphore_signal(barrier, inc=1, device_id=(g, lax.rem(p + i, pn)), device_id_type=MESH)
    pl.semaphore_wait(barrier, pn - 1 + 4 + zh)
    for k in (1, 2, 3):
        @pl.when(zh - k >= 0)
        def _():
            pl.semaphore_signal(zready.at[k - 1], inc=1, device_id=(zpeer(-k), p), device_id_type=MESH)

    for load in loads[:2]:
        load.wait()

    def zcopy(k, h):
        return remote(
            tall[h].at[g], tall[h].at[g], zs.at[k - 1, h], zr.at[k - 1, h], zpeer(k), p
        )

    def zup(k, where=True):
        @pl.when((zh + k < ZN) & where)
        def _():
            pl.semaphore_wait(zready.at[k - 1], 1)
            zcopy(k, UPPER).start()
            zcopy(k, LOWER).start()

    for h in (UPPER, LOWER):
        for k in (1, 3, 2):
            @pl.when(zh + k >= ZN)
            def _():
                zcopy(k, h).start()

    first = jnp.where(zh % 2 == 0, 3, 1)
    kinds = (0, first, 4 - first, 2)

    def ycopy(d, c, here, there, h):
        sign = 1 if d == RIGHT else -1
        piece = tall[h].at[slot(-sign * here, kinds[c])]
        src = piece
        return remote(
            src, piece, ys.at[d, there - 1, c, h], yr.at[d, there - 1, c, h], ypeer(sign * (there - here)), p
        )

    def along(c):
        return (UPPER,) if c in (1, 2) else (UPPER, LOWER)

    def await_piece(sem):
        pltpu.make_async_copy(tall_u.at[0], tall_u.at[0], sem).wait()

    near, far = (2, -2, 1, -1), (4, 3, -3)

    def bundle(k, planes, where):
        @pl.when(where)
        def _():
            for d in planes:
                piece = tall_l.at[slot(d, 0)]
                remote(piece, piece, bs.at[k // 2], br.at[k // 2], zpeer(k), p).start()

    def bundles(which):
        if which == "down":
            bundle(1, near, zh + 1 >= ZN)
            bundle(3, near, zh > 0)
        elif which == "up":
            bundle(1, near, zh + 1 < ZN)
            bundle(3, near, zh == 0)
        else:
            bundle(1, far, zh >= 0)
            bundle(3, far, zh >= 0)

    def bundle_wait(sem):
        size = (len(near) + len(far)) * part
        pltpu.make_async_copy(res.at[pl.ds(0, size), :], res.at[pl.ds(0, size), :], sem).wait()

    def onward(c, here, h):
        for d in (RIGHT, LEFT):
            for there in range(reach(d, c, h), here, -1):
                if here in (0, 2) and there <= here + 2:
                    ycopy(d, c, here, there, h).start()

    def zgot(c, h):
        await_piece(zr.at[kinds[c] - 1, h])
        if h in along(c):
            onward(c, 0, h)

    def ygot(c, here, h):
        for d in (RIGHT, LEFT):
            if here <= reach(d, c, h):
                await_piece(yr.at[d, here - 1, c, h])
        onward(c, here, h)

    onward(0, 0, LOWER)
    onward(0, 0, UPPER)

    def gcopy(i):
        j = turn(i, p)
        return j, remote(
            grad_ref.at[0, :, pl.ds(pl.multiple_of(j * blk, blk), blk)],
            gbuf.at[own_rows, :], gs.at[i], gr, g, owner_device(j),
        )

    for i in range(jn):
        j, copy = gcopy(i)

        @pl.when(owner_device(j) != p)
        def _():
            copy.start()

    @pl.when(active)
    def _():
        pltpu.make_async_copy(
            grad_ref.at[0, :, pl.ds(pl.multiple_of(mine * blk, blk), blk)], gbuf.at[own_rows, :], gr
        ).start()

    for load in loads[2:]:
        load.wait()
    layer = layer_ref[0]

    def prepare(n):
        part = slice(n * (blk // 4), (n + 1) * (blk // 4))

        @pl.when(active)
        def _():
            obt[:, part] = obuf[part, :].T
            spread = jnp.broadcast_to(ov_ref[...], (blk // 4, blk)).T
            values = iv_ref[:, pl.ds(pl.multiple_of(mine * blk + n * (blk // 4), blk // 4), blk // 4)]
            values = jnp.where(layer == 0, values[0:1], values[1:2])
            rbuf[:, part] = 1.0 / (spread * values + DAMPING)

    def project(n):
        lo, size = n * (blk // 4), blk // 4

        @pl.when(active)
        def _():
            if lo == 0:
                pltpu.make_async_copy(gbuf, gbuf, gr).wait()
            ybuf[lo : lo + size, :] = dot(obt[lo : lo + size, :], gbuf[...], ((1,), (0,))).astype(jnp.bfloat16)

    def tcopy(i, h):
        j = turn(i, p)
        return j, remote(tsend[h].at[j], tbuf.at[half_rows(h), :], ts.at[i, h], tr.at[h], g, owner_device(j))

    def owners(h):
        for i in range(jn):
            j, copy = tcopy(i, h)
            tsend[h][j] = tall[h][owner_ref[layer, j]]

            @pl.when(owner_device(j) != p)
            def _():
                copy.start()

        @pl.when(active)
        def _():
            pltpu.make_async_copy(tsend[h].at[mine], tbuf.at[half_rows(h), :], tr.at[h]).start()

    for step in ORDER:
        what, n = step[0], step[1]
        if what == "up":
            zup(n, eval_where(step[2], zh))
        elif what == "z":
            zgot(n, step[2])
        elif what == "y":
            ygot(n, step[2], step[3])
        elif what == "bundle":
            bundles(n)
        elif what == "bundled":
            bundle_wait(br.at[n // 2])
        elif what == "prepare":
            prepare(n)
        elif what == "project":
            project(n)
        else:
            owners(n)

    def mcopy(dest):
        strip = pl.ds(pl.multiple_of(dest * rows, rows), rows)
        cols = pl.ds(pl.multiple_of(mine * blk, blk), blk)
        return res.at[strip, :], out_ref.at[0, :, cols]

    half = blk // 2
    parts = 2
    size, targets = blk // parts, pn // parts

    @pl.when(active)
    def _():
        tops = [pl.ds(h * half, half) for h in (UPPER, LOWER)]
        for h in (UPPER, LOWER):
            pltpu.make_async_copy(tbuf.at[tops[h], :], tbuf.at[tops[h], :], tr.at[h]).wait()
            for lo in (0, half):
                some = slice(lo, lo + half)
                product = dot(ybuf[some, tops[h]], tbuf[tops[h], :], ((1,), (0,)))
                if h == UPPER:
                    xbuf[some, :] = product
                else:
                    sbuf[some, :] = ((xbuf[some, :] + product) * rbuf[some, :]).astype(jnp.bfloat16)
        for n in range(parts):
            turn = n
            part = pl.ds(pl.multiple_of(turn * size, size), size)
            mixed = dot(obuf[part, :], sbuf[...], ((1,), (0,))).astype(jnp.bfloat16)
            res[part, :] = dot(mixed, tbuf[...], ((1,), (1,))).astype(jnp.bfloat16)
            for i in sorted(range(targets), key=lambda i: i // 2 % 2):
                dest = turn * targets + i
                src, dst = mcopy(dest)

                @pl.when(dest != p)
                def _():
                    remote(src, dst, ms.at[dest], mr, g, dest).start()

                @pl.when(dest == p)
                def _():
                    pltpu.make_async_copy(src, dst, mr).start()

    pltpu.make_async_copy(out_ref.at[0], out_ref.at[0], mr).wait()

    for h in (UPPER, LOWER):
        for k in (1, 2, 3):
            await_piece(zs.at[k - 1, h])
        for c in range(ZN):
            for d in (RIGHT, LEFT):
                for there in range(1, reach(d, c, h) + 1):
                    if h in along(c):
                        await_piece(ys.at[d, there - 1, c, h])
    for k in (1, 3):
        bundle_wait(bs.at[k // 2])
    for i in range(jn):
        j, copy = gcopy(i)

        @pl.when(owner_device(j) != p)
        def _():
            copy.wait_send()
            for h in (UPPER, LOWER):
                await_piece(ts.at[i, h])

    @pl.when(active)
    def _():
        for i in range(pn):
            src, dst = mcopy(i)

            @pl.when(i != p)
            def _():
                remote(src, dst, ms.at[i], mr, g, i).wait_send()


def solution(mesh):
    yn = mesh.shape["grad"] // ZN
    pn = mesh.shape["dp"]

    def shards(gradient, out_bases, in_bases, out_values, in_values, block_layer, in_owner):
        rows, width = gradient.shape[1:]
        blk = out_bases.shape[1]
        jn = width // blk
        slots = yn * ZN
        bf16, f32 = jnp.bfloat16, jnp.float32
        any_spec = pl.BlockSpec(memory_space=pl.ANY)
        vmem = pl.BlockSpec(memory_space=pltpu.VMEM)
        dma = pltpu.SemaphoreType.DMA

        def body(*refs):
            kernel(yn, pn, jn, *refs)

        return pl.pallas_call(
            body,
            out_shape=pltpu.VMEM(gradient.shape, bf16),
            in_specs=[any_spec] * 7,
            out_specs=vmem,
            scratch_shapes=[
                pltpu.SMEM(in_owner.shape, jnp.int32),
                pltpu.SMEM(block_layer.shape, jnp.int32),
                pltpu.VMEM(out_values.shape, f32),
                pltpu.VMEM(in_values.shape, f32),
                pltpu.VMEM((blk, blk), bf16),
                pltpu.VMEM((blk, blk), bf16),
                pltpu.VMEM((blk, blk), bf16),
                pltpu.VMEM((blk, blk), bf16),
                pltpu.VMEM((blk, blk), f32),
                pltpu.VMEM((blk, blk), f32),
                pltpu.VMEM((slots, rows // 2, blk), bf16),
                pltpu.VMEM((slots, rows // 2, blk), bf16),
                pltpu.VMEM((jn, rows // 2, blk), bf16),
                pltpu.VMEM((jn, rows // 2, blk), bf16),
                pltpu.VMEM((blk, blk), bf16),
                pltpu.VMEM((blk, blk), bf16),
                pltpu.VMEM((blk, blk), bf16),
                dma((7,)),
                pltpu.SemaphoreType.REGULAR((ZN - 1,)),
                dma((ZN - 1, 2)),
                dma((ZN - 1, 2)),
                dma((2,)),
                dma((2,)),
                dma((2, 4, ZN, 2)),
                dma((2, 4, ZN, 2)),
                dma((jn,)),
                dma,
                dma((jn, 2)),
                dma((2,)),
                dma((pn,)),
                dma,
            ],
            compiler_params=pltpu.CompilerParams(
                collective_id=0, has_side_effects=True, vmem_limit_bytes=60 * 1024 * 1024
            ),
        )(in_owner, block_layer, gradient, out_bases, in_bases, out_values, in_values)

    in_specs = (
        P("grad", "dp", None),
        P("grad", None, None),
        P("grad", None, None),
        P("grad", None),
        P(),
        P("grad"),
        P(),
    )
    return jax.shard_map(shards, mesh=mesh, in_specs=in_specs, out_specs=P("grad", "dp", None), check_vma=False)
```
